128 devices in a mesh: dp: 8 (over z, core), own: 16 (over x, y).
Axes of the slice: x: 4, y: 4, z: 4, core: 2. Of those that a mesh axis runs over, the one named last changes fastest.
Arguments:
- queries: float32 [262144, 128], P(('dp', 'own')), may hold values from -24 to 24
- positives: float32 [262144, 128], P(('dp', 'own')), may hold values from -6 to 6
- neg_ids: int32 [2048, 512], P(('dp', 'own')), may hold values from 0 to 131071, as said below
- table: float32 [131072, 128], P('own'), may hold values from -6 to 6
- accum: float32 [131072, 128], P('own'), may hold values from 1e-07 to 1e-05
Outputs:
- new_table: float32 [131072, 128], P('own')
- query_grad: float32 [262144, 128], P(('dp', 'own'))
The draws below stay inside these ranges and needn't reach their ends.
Inputs may be any that keep to these rules, and one draw needn't show every extreme that they name: Row r of neg_ids holds rows of owner r % 16 only: ids from (r % 16) * 8192 to (r % 16 + 1) * 8192 - 1. Every row holds exactly 256 distinct ids, each appearing one or more times.
All inputs are finite; a program needn't handle non-finite values.
Results may differ from the reference program's by a relative error of at most 0.0003.
Values sent between devices are 32-bit elements; how exact they have to be, the bound alone decides.
A program may use at most 128 MiB of HBM per device.

```python
import math
import jax
import jax.numpy as jnp
from jax import lax

E = 128
Q_DEV = 2048
NEG_DEV = 8192
ROWS_DEV = 8192
ITEMS = 131072
TOKENS = 262144
PER = 512
FEW = 256
N_DP = 8
N_OWN = 16


def shared_normal(key):
    return jnp.clip(jax.random.normal(key, (TOKENS, E), jnp.float32), -6.0, 6.0)


def draw_positives(key, part):
    base = shared_normal(key)
    return base


def draw_queries(key, part):
    key = jax.random.fold_in(key, 2)
    own_part = jnp.clip(jax.random.normal(key, (TOKENS, E), jnp.float32), -6.0, 6.0) * E ** (-0.5)
    return own_part


def draw_neg_ids(key, part):
    key = jax.random.fold_in(key, 3)
    rows = N_DP * N_OWN * N_OWN
    owner = (jnp.arange(rows) % N_OWN)[:, None]
    stride = ROWS_DEV // FEW
    key_a, key_b, key_c, key_d = jax.random.split(key, 4)
    jitter = jax.random.randint(key_a, (rows, FEW), 0, stride)
    rotate = jax.random.randint(key_b, (rows, 1), 0, ROWS_DEV)
    distinct = (jnp.arange(FEW)[None, :] * stride + jitter + rotate) % ROWS_DEV
    popular = max(1, FEW // 8)
    extra = jax.random.randint(key_c, (rows, PER - FEW), 0, popular)
    every = jnp.broadcast_to(jnp.arange(FEW)[None, :], (rows, FEW))
    picks = jnp.concatenate([every, extra], axis=1)
    picks = jax.random.permutation(key_d, picks, axis=1, independent=True)
    local = jnp.take_along_axis(distinct, picks, axis=1)
    return (owner * ROWS_DEV + local).astype(jnp.int32)


def level_of(own_key, extent, cuts, least, largest):
    def one(axis_at, blocks):
        draws = jax.random.uniform(jax.random.fold_in(jax.random.fold_in(own_key, 6), axis_at), (blocks,), jnp.float32, least / len(cuts), largest / len(cuts))
        return jnp.repeat(jnp.exp(draws), extent[axis_at] // blocks).reshape((-1,) + (1,) * (len(extent) - axis_at - 1))

    level = one(*cuts[0])
    for cut in cuts[1:]:
        level = level * one(*cut)
    return level


def normal_values(own_key, extent, spread, reach, cuts=(), kind=jnp.bfloat16):
    array = jax.random.normal(own_key, extent, jnp.float32) * spread
    if len(cuts) > 0:
        array = level_of(own_key, extent, cuts, -0.22, 0.18) * array
    return jnp.clip(array, min=-reach, max=reach).astype(kind)


def setup_inputs(seed: int = 0) -> dict:
    keys = jax.random.split(jax.random.key(seed), 6)
    queries = draw_queries(jax.random.fold_in(keys[5], 71), 0)
    positives = draw_positives(jax.random.fold_in(keys[5], 71), 0)
    neg_ids = draw_neg_ids(jax.random.fold_in(keys[5], 71), 0)
    table = normal_values(keys[3], (ITEMS, E), 1.0, 6.0, ((0, 16),), jnp.float32)
    accum = jnp.clip(jnp.exp(math.log(9.999999747378752e-06) - 4.6051701 * jax.random.uniform(keys[4], (ITEMS, E), jnp.float32) ** level_of(keys[4], (ITEMS, E), ((0, 16),), -0.2, 0.2)), 1.0000000116860974e-07, 9.999999747378752e-06)
    return {"queries": queries, "positives": positives, "neg_ids": neg_ids, "table": table, "accum": accum}


def one_device(table, query_rows, positive_rows, ids):
    neg_rows = table[ids]
    pos_score = lax.optimization_barrier(jnp.sum(query_rows * positive_rows, axis=1))
    neg_scores = jnp.dot(query_rows, neg_rows.T, precision=lax.Precision.HIGHEST)
    top = jnp.maximum(pos_score, lax.optimization_barrier(jnp.max(neg_scores, axis=1)))
    pos_exp = jnp.exp(pos_score - top)
    neg_exp = jnp.exp(neg_scores - top[:, None])
    total = pos_exp + lax.optimization_barrier(jnp.sum(neg_exp, axis=1))
    pos_dz = pos_exp / total - 1.0
    neg_dz = neg_exp / total[:, None]
    query_grad = pos_dz[:, None] * positive_rows + jnp.dot(neg_dz, neg_rows, precision=lax.Precision.HIGHEST)
    neg_grad = jnp.dot(neg_dz.T, query_rows, precision=lax.Precision.HIGHEST)
    return (query_grad, neg_grad)

def reference(queries, positives, neg_ids, table, accum):
    devices = N_DP * N_OWN
    query_blocks = queries.reshape(devices, Q_DEV, E)
    positive_blocks = positives.reshape(devices, Q_DEV, E)
    id_blocks = neg_ids.reshape(devices, NEG_DEV)

    def step(grad, items):
        query_rows, positive_rows, ids = items
        query_grad, neg_grad = one_device(table, query_rows, positive_rows, ids)
        grad = grad + jax.ops.segment_sum(neg_grad, ids, num_segments=ITEMS)
        return (grad, query_grad)
    grad, query_grad = lax.scan(step, jnp.zeros((ITEMS, E), jnp.float32), (query_blocks, positive_blocks, id_blocks))
    new_accum = accum + grad * grad
    new_table = table - 0.5 * grad / (jnp.sqrt(new_accum) + 1e-08)
    return (new_table, query_grad.reshape(TOKENS, E))
```

```python
import functools
import jax
import jax.numpy as jnp
from jax import lax
from jax.experimental import pallas as pl
from jax.experimental.pallas import tpu as pltpu
from jax.sharding import PartitionSpec as P

F32, BF16, I32 = jnp.float32, jnp.bfloat16, jnp.int32
LOG2E = 1.4426950408889634
MIB = 1024 * 1024


def split(x):
    hi = x.astype(BF16)
    return hi, (x - hi.astype(F32)).astype(BF16)


def dot(a, b):
    return lax.dot_general(a, b, (((1,), (0,)), ((), ())), preferred_element_type=F32)


def dot_t(a, b):
    return lax.dot_general(a, b, (((1,), (1,)), ((), ())), preferred_element_type=F32)


def dedup_kernel(rows_dev, ids_ref, out_ref, cnt_ref):
    owners, per = ids_ref.shape
    few = 256
    base = lax.broadcasted_iota(I32, (owners, per), 0) * rows_dev
    local = (ids_ref[...] - base).astype(F32)
    cols = jnp.transpose(jnp.concatenate([local, jnp.zeros((128 - owners, per), F32)], axis=0))
    lane = lax.broadcasted_iota(I32, (128, per), 1)
    sub = lax.broadcasted_iota(I32, (128, per), 0)
    firsts, counts = [], []
    for r in range(owners):
        row = local[r : r + 1, :]
        count = jnp.zeros((1, per), F32)
        before = jnp.zeros((1, per), F32)
        for b in range(per // 128):
            col = cols[b * 128 : (b + 1) * 128, r : r + 1]
            eq = jnp.where(col == row, 1.0, 0.0)
            count = count + jnp.sum(eq, axis=0, keepdims=True)
            before = before + jnp.sum(jnp.where(sub + b * 128 < lane, eq, 0.0), axis=0, keepdims=True)
        firsts.append(before < 0.5)
        counts.append(count)
    first = jnp.concatenate([jnp.where(f, 1.0, 0.0) for f in firsts], axis=0)
    count = jnp.concatenate(counts, axis=0)
    tri = jnp.where(
        lax.broadcasted_iota(I32, (per, per), 0) < lax.broadcasted_iota(I32, (per, per), 1), 1.0, 0.0
    ).astype(BF16)
    place = dot(first.astype(BF16), tri)
    place = jnp.where(first > 0.5, place, -1.0).astype(I32)
    li = local.astype(I32)
    ci = count.astype(I32)
    parts = [(li >> 7).astype(F32), (li & 127).astype(F32), (ci >> 4).astype(F32), (ci & 15).astype(F32)]
    slot = lax.broadcasted_iota(I32, (few, per), 0)
    for r in range(owners):
        hot = jnp.where(slot == place[r : r + 1, :], 1.0, 0.0).astype(BF16)
        vals = jnp.concatenate([p[r : r + 1, :] for p in parts] + [jnp.zeros((12, per), F32)], axis=0)
        got = dot_t(vals.astype(BF16), hot)
        ids = got[0:1, :] * 128.0 + got[1:2, :]
        cnt = got[2:3, :] * 16.0 + got[3:4, :]
        both = jnp.concatenate([ids[:, :128], ids[:, 128:], jnp.zeros((6, 128), F32)], axis=0)
        out_ref[r] = both.astype(I32)
        cnt_ref[r] = jnp.broadcast_to(cnt, (8, few))


def dedup(ids, rows_dev):
    owners, per = ids.shape
    return pl.pallas_call(
        functools.partial(dedup_kernel, rows_dev),
        out_shape=(
            jax.ShapeDtypeStruct((owners, 8, 128), I32),
            jax.ShapeDtypeStruct((owners, 8, 256), F32),
        ),
        in_specs=[pl.BlockSpec(memory_space=pltpu.VMEM)],
        out_specs=(pl.BlockSpec(memory_space=pltpu.VMEM),) * 2,
        compiler_params=pltpu.CompilerParams(vmem_limit_bytes=16 * MIB),
        name="dedup",
    )(ids)


def gather_kernel(ids_ref, table_ref, out_ref):
    few = out_ref.shape[1]

    def block(s, c):
        def group(g, c):
            for i in range(16):
                j = g * 16 + i
                out_ref[s, pl.ds(j, 1), :] = table_ref[pl.ds(ids_ref[s, j >> 7, j & 127], 1), :]
            return c
        return lax.fori_loop(0, few // 16, group, c)

    lax.fori_loop(0, out_ref.shape[0], block, 0)


def gather(ids, table):
    return pl.pallas_call(
        gather_kernel,
        out_shape=jax.ShapeDtypeStruct((ids.shape[0], 256, 128), F32),
        in_specs=[pl.BlockSpec(memory_space=pltpu.SMEM), pl.BlockSpec(memory_space=pltpu.VMEM)],
        out_specs=pl.BlockSpec(memory_space=pltpu.VMEM),
        compiler_params=pltpu.CompilerParams(vmem_limit_bytes=32 * MIB),
        name="gather",
    )(ids, table)


def scatter_kernel(ids_ref, grad_ref, out_ref):
    few = grad_ref.shape[1]
    out_ref[...] = jnp.zeros_like(out_ref)

    def block(s, c):
        def group(g, c):
            at, vals = [], []
            for i in range(16):
                j = g * 16 + i
                at.append(ids_ref[s, j >> 7, j & 127])
                vals.append(out_ref[pl.ds(at[i], 1), :] + grad_ref[s, pl.ds(j, 1), :])
            for i in range(16):
                out_ref[pl.ds(at[i], 1), :] = vals[i]
            return c
        return lax.fori_loop(0, few // 16, group, c)

    lax.fori_loop(0, grad_ref.shape[0], block, 0)


def scatter(ids, grads, rows_dev):
    return pl.pallas_call(
        scatter_kernel,
        out_shape=jax.ShapeDtypeStruct((rows_dev, 128), F32),
        in_specs=[pl.BlockSpec(memory_space=pltpu.SMEM), pl.BlockSpec(memory_space=pltpu.VMEM)],
        out_specs=pl.BlockSpec(memory_space=pltpu.VMEM),
        compiler_params=pltpu.CompilerParams(vmem_limit_bytes=32 * MIB),
        name="scatter",
    )(ids, grads)


def prepare(q_ref, p_ref, qtf, ptf, qt2, m, total, qacc):
    count = q_ref.shape[0]
    for t in range(count // 128):
        tile = pl.ds(t * 128, 128)
        qt = jnp.transpose(q_ref[tile, :])
        pt = jnp.transpose(p_ref[tile, :])
        qtf[:, tile] = qt
        ptf[:, tile] = pt
        hi, lo = split(qt * LOG2E)
        qt2[0:128, tile] = hi
        qt2[128:256, tile] = lo
        m[0:1, tile] = jnp.sum(qt * pt, axis=0, keepdims=True) * LOG2E
    total[...] = jnp.ones_like(total)
    qacc[...] = ptf[...]


def phase_a(n, w, s, qt2, m, ms, total, qacc, eh, el, tq):
    hi, lo = split(n)
    nt = jnp.transpose(n) * w
    nth, ntl = split(nt)
    wh, wl = split(w)
    sub = lax.broadcasted_iota(I32, (16, 256), 0)
    wrows = jnp.where(sub == 0, wh.astype(F32), jnp.where(sub == 1, wl.astype(F32), 0.0)).astype(BF16)
    left1 = jnp.concatenate([nth, wrows, ntl], axis=0)
    left2 = left1[0:144]
    n1 = jnp.concatenate([hi, hi], axis=1)
    n2 = jnp.concatenate([lo, lo], axis=1)
    count = qt2.shape[1]
    for t in range(count // tq):
        tile = pl.ds(t * tq, tq)
        right = qt2[:, tile]
        score = dot(n1, right) + dot(n2, right)
        old = m[0:1, tile]
        new = jnp.maximum(old, jnp.max(score, axis=0, keepdims=True))
        alpha = jnp.exp2(old - new)
        m[0:1, tile] = new
        ms[s, 0:1, tile] = new
        e = jnp.exp2(score - new)
        h, l = split(e)
        eh[s, :, tile] = h
        el[s, :, tile] = l
        a1 = dot(left1, h)
        a2 = dot(left2, l)
        total[0:1, tile] = (
            total[0:1, tile] * alpha + (a1[128:129] + a1[129:130]) + (a2[128:129] + a2[129:130])
        )
        qacc[:, tile] = qacc[:, tile] * alpha + (a1[0:128] + (a1[144:272] + a2[0:128]))


def finish(qg_ref, ptf, m, total, qacc):
    count = qacc.shape[1]
    for t in range(count // 128):
        tile = pl.ds(t * 128, 128)
        g = qacc[:, tile] * (1.0 / total[0:1, tile]) - ptf[:, tile]
        qg_ref[tile, :] = jnp.transpose(g)


def phase_b(w, s, qtf, m, ms, total, eh, el):
    c = jnp.exp2(ms[s, 0:1, :] - m[0:1, :]) * (1.0 / total[0:1, :])
    qh, ql = split(qtf[...] * c)
    g1 = dot_t(eh[s], jnp.concatenate([qh, ql], axis=0))
    g2 = dot_t(el[s], qh)
    wc = jnp.transpose(jnp.broadcast_to(w, (128, 256)))
    return wc * (g1[:, 0:128] + (g1[:, 128:256] + g2))


def compute_kernel(tq, q_ref, p_ref, n_ref, w_ref, qg_ref, g_ref, qtf, ptf, qt2, m, ms, total, qacc, eh, el):
    prepare(q_ref, p_ref, qtf, ptf, qt2, m, total, qacc)

    def a(s, c):
        phase_a(n_ref[s], w_ref[s, 0:1, :], s, qt2, m, ms, total, qacc, eh, el, tq)
        return c

    lax.fori_loop(0, n_ref.shape[0], a, 0)
    finish(qg_ref, ptf, m, total, qacc)

    def b(s, c):
        g_ref[s] = phase_b(w_ref[s, 0:1, :], s, qtf, m, ms, total, eh, el)
        return c

    lax.fori_loop(0, n_ref.shape[0], b, 0)


def compute_scratch(count, owners):
    return [
        pltpu.VMEM((128, count), F32),
        pltpu.VMEM((128, count), F32),
        pltpu.VMEM((256, count), BF16),
        pltpu.VMEM((8, count), F32),
        pltpu.VMEM((owners, 8, count), F32),
        pltpu.VMEM((8, count), F32),
        pltpu.VMEM((128, count), F32),
        pltpu.VMEM((owners, 256, count), BF16),
        pltpu.VMEM((owners, 256, count), BF16),
    ]


def compute(q, p, n, w, tq=512):
    count, owners = q.shape[0], n.shape[0]
    vm = pl.BlockSpec(memory_space=pltpu.VMEM)
    return pl.pallas_call(
        functools.partial(compute_kernel, tq),
        out_shape=(jax.ShapeDtypeStruct((count, 128), F32), jax.ShapeDtypeStruct((owners, 256, 128), F32)),
        in_specs=[vm] * 4,
        out_specs=(vm, vm),
        scratch_shapes=compute_scratch(count, owners),
        compiler_params=pltpu.CompilerParams(vmem_limit_bytes=60 * MIB),
        name="compute",
    )(q, p, n, w)


def adagrad(table_rows, accum_rows, grad):
    new_accum = accum_rows + grad * grad
    return table_rows - 0.5 * grad / (jnp.sqrt(new_accum) + 1e-08)


def local(queries, positives, neg_ids, table, accum):
    ids, counts = dedup(neg_ids, table.shape[0])
    received = lax.all_to_all(ids, "own", split_axis=0, concat_axis=0, tiled=True)
    rows = lax.all_to_all(gather(received, table), "own", split_axis=0, concat_axis=0, tiled=True)
    query_grad, neg_grad = compute(queries, positives, rows, counts)
    arrived = lax.all_to_all(neg_grad, "own", split_axis=0, concat_axis=0, tiled=True)
    dense = scatter(received, arrived, table.shape[0])
    summed = lax.psum(dense, "dp")
    return (adagrad(table, accum, summed), query_grad)


def solution(mesh):
    return jax.shard_map(
        local,
        mesh=mesh,
        in_specs=(
            P(("dp", "own"), None),
            P(("dp", "own"), None),
            P(("dp", "own"), None),
            P("own", None),
            P("own", None),
        ),
        out_specs=(P("own", None), P(("dp", "own"), None)),
        check_vma=False,
    )
```

```python
import functools
import jax
import jax.numpy as jnp
from jax import lax
from jax.experimental import pallas as pl
from jax.experimental.pallas import tpu as pltpu
from jax.sharding import PartitionSpec as P

F32, BF16, I32 = jnp.float32, jnp.bfloat16, jnp.int32
LOG2E = 1.4426950408889634
MIB = 1024 * 1024


def split(x):
    hi = x.astype(BF16)
    return hi, (x - hi.astype(F32)).astype(BF16)


def dot(a, b):
    return lax.dot_general(a, b, (((1,), (0,)), ((), ())), preferred_element_type=F32)


def dot_t(a, b):
    return lax.dot_general(a, b, (((1,), (1,)), ((), ())), preferred_element_type=F32)


def dedup_kernel(rows_dev, ids_ref, out_ref, cnt_ref):
    owners, per = ids_ref.shape
    few = 256
    base = lax.broadcasted_iota(I32, (owners, per), 0) * rows_dev
    local = (ids_ref[...] - base).astype(F32)
    cols = jnp.transpose(jnp.concatenate([local, jnp.zeros((128 - owners, per), F32)], axis=0))
    lane = lax.broadcasted_iota(I32, (128, per), 1)
    sub = lax.broadcasted_iota(I32, (128, per), 0)
    firsts, counts = [], []
    for r in range(owners):
        row = local[r : r + 1, :]
        count = jnp.zeros((1, per), F32)
        before = jnp.zeros((1, per), F32)
        for b in range(per // 128):
            col = cols[b * 128 : (b + 1) * 128, r : r + 1]
            eq = jnp.where(col == row, 1.0, 0.0)
            count = count + jnp.sum(eq, axis=0, keepdims=True)
            before = before + jnp.sum(jnp.where(sub + b * 128 < lane, eq, 0.0), axis=0, keepdims=True)
        firsts.append(before < 0.5)
        counts.append(count)
    first = jnp.concatenate([jnp.where(f, 1.0, 0.0) for f in firsts], axis=0)
    count = jnp.concatenate(counts, axis=0)
    tri = jnp.where(
        lax.broadcasted_iota(I32, (per, per), 0) < lax.broadcasted_iota(I32, (per, per), 1), 1.0, 0.0
    ).astype(BF16)
    place = dot(first.astype(BF16), tri)
    place = jnp.where(first > 0.5, place, -1.0).astype(I32)
    li = local.astype(I32)
    ci = count.astype(I32)
    parts = [(li >> 7).astype(F32), (li & 127).astype(F32), (ci >> 4).astype(F32), (ci & 15).astype(F32)]
    slot = lax.broadcasted_iota(I32, (few, per), 0)
    for r in range(owners):
        hot = jnp.where(slot == place[r : r + 1, :], 1.0, 0.0).astype(BF16)
        vals = jnp.concatenate([p[r : r + 1, :] for p in parts] + [jnp.zeros((12, per), F32)], axis=0)
        got = dot_t(vals.astype(BF16), hot)
        ids = got[0:1, :] * 128.0 + got[1:2, :]
        cnt = got[2:3, :] * 16.0 + got[3:4, :]
        both = jnp.concatenate([ids[:, :128], ids[:, 128:], jnp.zeros((6, 128), F32)], axis=0)
        out_ref[r] = both.astype(I32)
        cnt_ref[r] = jnp.broadcast_to(cnt, (8, few))


def dedup(ids, rows_dev):
    owners, per = ids.shape
    return pl.pallas_call(
        functools.partial(dedup_kernel, rows_dev),
        out_shape=(
            jax.ShapeDtypeStruct((owners, 8, 128), I32),
            jax.ShapeDtypeStruct((owners, 8, 256), F32),
        ),
        in_specs=[pl.BlockSpec(memory_space=pltpu.VMEM)],
        out_specs=(pl.BlockSpec(memory_space=pltpu.VMEM),) * 2,
        compiler_params=pltpu.CompilerParams(vmem_limit_bytes=16 * MIB),
        name="dedup",
    )(ids)


def scatter_kernel(ids_ref, grad_ref, out_ref):
    out_ref[...] = jnp.zeros_like(out_ref)

    def block(k, c):
        s, h = k // 2, k % 2
        for b in range(8):
            at = [pl.ds(ids_ref[s, h, b * 16 + i], 1) for i in range(16)]
            vals = [out_ref[at[i], :] + grad_ref[s, pl.ds(h * 128 + b * 16 + i, 1), :] for i in range(16)]
            for i in range(16):
                out_ref[at[i], :] = vals[i]
        return c

    lax.fori_loop(0, 2 * grad_ref.shape[0], block, 0)


def scatter(ids, grads, rows_dev):
    return pl.pallas_call(
        scatter_kernel,
        out_shape=jax.ShapeDtypeStruct((rows_dev, 128), F32),
        in_specs=[pl.BlockSpec(memory_space=pltpu.SMEM), pl.BlockSpec(memory_space=pltpu.VMEM)],
        out_specs=pl.BlockSpec(memory_space=pltpu.VMEM),
        compiler_params=pltpu.CompilerParams(vmem_limit_bytes=32 * MIB),
        name="scatter",
    )(ids, grads)


def prepare(q_ref, p_ref, qtf, ptf, qt2, m, total, qacc):
    count = q_ref.shape[0]
    for t in range(count // 128):
        tile = pl.ds(t * 128, 128)
        qt = jnp.transpose(q_ref[tile, :])
        pt = jnp.transpose(p_ref[tile, :])
        qtf[:, tile] = qt
        ptf[:, tile] = pt
        hi, lo = split(qt * LOG2E)
        qt2[0:128, tile] = hi
        qt2[128:256, tile] = lo
        m[0:1, tile] = jnp.sum(qt * pt, axis=0, keepdims=True) * LOG2E
    total[...] = jnp.ones_like(total)
    qacc[...] = ptf[...]


def phase_a(n, w, s, qt2, m, ms, total, qacc, eh, el, tq):
    hi, lo = split(n)
    nt = jnp.transpose(n) * w
    nth, ntl = split(nt)
    wh, wl = split(w)
    sub = lax.broadcasted_iota(I32, (16, 256), 0)
    wrows = jnp.where(sub == 0, wh.astype(F32), jnp.where(sub == 1, wl.astype(F32), 0.0)).astype(BF16)
    left1 = jnp.concatenate([nth, wrows, ntl], axis=0)
    left2 = left1[0:144]
    n1 = jnp.concatenate([hi, hi], axis=1)
    n2 = jnp.concatenate([lo, lo], axis=1)
    count = qt2.shape[1]
    for t in range(count // tq):
        tile = pl.ds(t * tq, tq)
        right = qt2[:, tile]
        score = dot(n1, right) + dot(n2, right)
        old = m[0:1, tile]
        new = jnp.maximum(old, jnp.max(score, axis=0, keepdims=True))
        alpha = jnp.exp2(old - new)
        m[0:1, tile] = new
        ms[s, 0:1, tile] = new
        e = jnp.exp2(score - new)
        h, l = split(e)
        eh[s, :, tile] = h
        el[s, :, tile] = l
        a1 = dot(left1, h)
        a2 = dot(left2, l)
        total[0:1, tile] = (
            total[0:1, tile] * alpha + (a1[128:129] + a1[129:130]) + (a2[128:129] + a2[129:130])
        )
        qacc[:, tile] = qacc[:, tile] * alpha + (a1[0:128] + (a1[144:272] + a2[0:128]))


def finish(qg_ref, ptf, m, total, qacc):
    count = qacc.shape[1]
    for t in range(count // 128):
        tile = pl.ds(t * 128, 128)
        g = qacc[:, tile] * (1.0 / total[0:1, tile]) - ptf[:, tile]
        qg_ref[tile, :] = jnp.transpose(g)


def phase_b(w, s, qtf, m, ms, total, eh, el):
    c = jnp.exp2(ms[s, 0:1, :] - m[0:1, :]) * (1.0 / total[0:1, :])
    qh, ql = split(qtf[...] * c)
    g1 = dot_t(eh[s], jnp.concatenate([qh, ql], axis=0))
    g2 = dot_t(el[s], qh)
    wc = jnp.transpose(jnp.broadcast_to(w, (128, 256)))
    return wc * (g1[:, 0:128] + (g1[:, 128:256] + g2))


def compute_scratch(count, owners):
    return [
        pltpu.VMEM((128, count), F32),
        pltpu.VMEM((128, count), F32),
        pltpu.VMEM((256, count), BF16),
        pltpu.VMEM((8, count), F32),
        pltpu.VMEM((owners, 8, count), F32),
        pltpu.VMEM((8, count), F32),
        pltpu.VMEM((128, count), F32),
        pltpu.VMEM((owners, 256, count), BF16),
        pltpu.VMEM((owners, 256, count), BF16),
    ]


def exchange_kernel(
    tq, ids_ref, cnt_ref, q_ref, p_ref, table_ref, qg_ref, idr_ref, arrived_ref,
    qtf, ptf, qt2, m, ms, total, qacc, eh, el,
    idr, ids_smem, sent, rows, gsent, wslot,
    ids_s, ids_r, row_s, row_r, grad_s, grad_r, local_s,
):
    owners = ids_ref.shape[0]
    me = lax.axis_index("own")
    x, y = me // 4, me % 4

    def up(s):
        dx, dy = s % 4, (s + s // 4) % 4
        return ((x + dx) % 4) * 4 + (y + dy) % 4

    def down(s):
        dx, dy = s % 4, (s + s // 4) % 4
        return ((x + 4 - dx) % 4) * 4 + (y + 4 - dy) % 4

    def remote(src, dst, send, recv, device):
        return pltpu.make_async_remote_copy(
            src_ref=src, dst_ref=dst, send_sem=send, recv_sem=recv,
            device_id={"own": device}, device_id_type=pl.DeviceIdType.MESH,
        )

    def ids_copy(s):
        return remote(ids_ref.at[up(s)], idr.at[s], ids_s.at[s], ids_r.at[s], up(s))

    def row_copy(s):
        return remote(sent.at[s], rows.at[s], row_s.at[s], row_r.at[s], down(s))

    def grad_copy(s):
        return remote(gsent.at[s], arrived_ref.at[s], grad_s.at[s], grad_r.at[s], up(s))

    def each(first, body):
        def step(s, c):
            body(s)
            return c

        lax.fori_loop(first, owners, step, 0)

    barrier = pltpu.get_barrier_semaphore()
    each(1, lambda s: pl.semaphore_signal(
        barrier, inc=1, device_id={"own": up(s)}, device_id_type=pl.DeviceIdType.MESH))
    pl.semaphore_wait(barrier, owners - 1)
    each(1, lambda s: ids_copy(s).start())
    idr[0] = ids_ref[me]

    def counts(s):
        wslot[s] = cnt_ref[up(s)]

    each(0, counts)
    prepare(q_ref, p_ref, qtf, ptf, qt2, m, total, qacc)
    each(1, lambda s: ids_copy(s).wait_recv())
    to_smem = pltpu.make_async_copy(idr, ids_smem, local_s.at[0])
    to_smem.start()
    idr_ref[...] = idr[...]
    to_smem.wait()

    def fetch(s, into):
        def half(h, c):
            for i in range(128):
                into[s, pl.ds(h * 128 + i, 1), :] = table_ref[pl.ds(ids_smem[s, h, i], 1), :]
            return c

        lax.fori_loop(0, 2, half, 0)

    def send_rows(s):
        fetch(s, sent)
        row_copy(s).start()

    each(1, send_rows)
    fetch(0, rows)

    def scores(s):
        @pl.when(s > 0)
        def _():
            row_copy(s).wait_recv()

        phase_a(rows[s], wslot[s, 0:1, :], s, qt2, m, ms, total, qacc, eh, el, tq)

    each(0, scores)

    def gradients(i):
        s = (i + 1) % owners
        gsent[s] = phase_b(wslot[s, 0:1, :], s, qtf, m, ms, total, eh, el)

        @pl.when(s > 0)
        def _():
            grad_copy(s).start()

    each(0, gradients)
    own = pltpu.make_async_copy(gsent.at[0], arrived_ref.at[0], local_s.at[1])
    own.start()
    finish(qg_ref, ptf, m, total, qacc)
    each(1, lambda s: ids_copy(s).wait_send())
    each(1, lambda s: row_copy(s).wait_send())
    each(1, lambda s: grad_copy(s).wait())
    own.wait()


def exchange(ids, counts, q, p, table, tq=512):
    count, owners = q.shape[0], ids.shape[0]
    vm = pl.BlockSpec(memory_space=pltpu.VMEM)
    dma = pltpu.SemaphoreType.DMA((owners,))
    return pl.pallas_call(
        functools.partial(exchange_kernel, tq),
        out_shape=(
            jax.ShapeDtypeStruct((count, 128), F32),
            jax.ShapeDtypeStruct(ids.shape, I32),
            jax.ShapeDtypeStruct((owners, 256, 128), F32),
        ),
        in_specs=[vm] * 5,
        out_specs=(vm, vm, pl.BlockSpec(memory_space=pl.ANY)),
        scratch_shapes=compute_scratch(count, owners)
        + [
            pltpu.VMEM(ids.shape, I32),
            pltpu.SMEM(ids.shape, I32),
            pltpu.VMEM((owners, 256, 128), F32),
            pltpu.VMEM((owners, 256, 128), F32),
            pltpu.VMEM((owners, 256, 128), F32),
            pltpu.VMEM(counts.shape, F32),
        ]
        + [dma] * 6
        + [pltpu.SemaphoreType.DMA((2,))],
        compiler_params=pltpu.CompilerParams(
            vmem_limit_bytes=60 * MIB, collective_id=0, has_side_effects=True
        ),
        name="exchange",
    )(ids, counts, q, p, table)


def update_kernel(
    d_ref, table_ref, accum_ref, out_ref,
    mine, other, ring, fresh, tab, acc,
    load_s, core_s, core_r, ring_s, ring_r, all_s, all_r, peer_s, peer_r,
):
    rows = d_ref.shape[0]
    half, ch = rows // 2, rows // 8
    hf = ch // 2
    dp = lax.axis_index("dp")
    z, c = dp // 2, dp % 2
    peer = z * 2 + (1 - c)
    nxt = ((z + 1) % 4) * 2 + c
    prv = ((z + 3) % 4) * 2 + c

    def remote(src, dst, send, recv, device):
        return pltpu.make_async_remote_copy(
            src_ref=src, dst_ref=dst, send_sem=send, recv_sem=recv,
            device_id={"dp": device}, device_id_type=pl.DeviceIdType.MESH,
        )

    def at(k, core, part=None):
        first = core * half + ((z + k) % 4) * ch
        if part is None:
            return pl.ds(pl.multiple_of(first, ch), ch)
        return pl.ds(pl.multiple_of(first + part * hf, hf), hf)

    loads = [pltpu.make_async_copy(d_ref.at[at(k, c)], mine.at[k], load_s.at[k]) for k in range(4)]
    loads.append(pltpu.make_async_copy(table_ref.at[at(0, c)], tab, load_s.at[4]))
    loads.append(pltpu.make_async_copy(accum_ref.at[at(0, c)], acc, load_s.at[5]))
    for k in (2, 1, 3, 0, 4, 5):
        loads[k].start()

    barrier = pltpu.get_barrier_semaphore()
    for device in (peer, nxt, prv):
        pl.semaphore_signal(barrier, inc=1, device_id={"dp": device}, device_id_type=pl.DeviceIdType.MESH)
    pl.semaphore_wait(barrier, 3)

    core = [remote(d_ref.at[at(k, 1 - c)], other.at[k], core_s.at[k], core_r.at[k], peer) for k in range(4)]
    for k in (2, 1, 3, 0):
        core[k].start()

    def pair(k):
        loads[k].wait()
        core[k].wait_recv()
        mine[k] = mine[k] + other[k]

    first, second = pl.ds(0, hf), pl.ds(hf, hf)

    def hop(i, k, part, device):
        return remote(mine.at[k, part], ring.at[i], ring_s.at[i], ring_r.at[i], device)

    hops = [
        hop(0, 2, first, nxt), hop(1, 2, second, prv),
        hop(2, 1, second, nxt), hop(3, 3, first, prv),
        hop(4, 1, first, nxt), hop(5, 3, second, prv),
    ]
    pair(2)
    hops[0].start()
    hops[1].start()
    pair(1)
    hops[2].start()
    pair(3)
    hops[3].start()
    hops[0].wait_recv()
    mine[1, first, :] = mine[1, first, :] + ring[0]
    hops[4].start()
    hops[1].wait_recv()
    mine[3, second, :] = mine[3, second, :] + ring[1]
    hops[5].start()
    pair(0)
    loads[4].wait()
    loads[5].wait()

    def adagrad(part, a, b):
        grad = mine[0, part, :] + (ring[a] + ring[b])
        new_accum = acc[part, :] + grad * grad
        fresh[part, :] = tab[part, :] - 0.5 * grad / (jnp.sqrt(new_accum) + 1e-08)

    def own_part(i, part, device):
        rows_ = at(0, c, part)
        return remote(fresh.at[pl.ds(part * hf, hf)], out_ref.at[rows_], all_s.at[i], all_r.at[i], device)

    def passed(i, k, part, device):
        rows_ = at(k, c, part)
        return remote(out_ref.at[rows_], out_ref.at[rows_], all_s.at[i], all_r.at[i], device)

    def to_peer(k, part):
        rows_ = at(k, c, part)
        src = fresh.at[pl.ds(part * hf, hf)] if k == 0 else out_ref.at[rows_]
        return remote(src, out_ref.at[rows_], peer_s.at[k, part], peer_r.at[k, part], peer)

    shares = [
        own_part(0, 0, nxt), own_part(1, 1, nxt), own_part(2, 0, prv), own_part(3, 1, prv),
        passed(4, 3, 0, nxt), passed(5, 1, 1, prv),
    ]
    peers = [[to_peer(k, part) for part in range(2)] for k in range(4)]
    keep = [
        pltpu.make_async_copy(fresh.at[pl.ds(part * hf, hf)], out_ref.at[at(0, c, part)], load_s.at[6 + part])
        for part in range(2)
    ]
    hops[3].wait_recv()
    hops[4].wait_recv()
    adagrad(first, 3, 4)
    shares[0].start()
    hops[2].wait_recv()
    hops[5].wait_recv()
    adagrad(second, 2, 5)
    shares[3].start()
    shares[1].start()
    shares[2].start()
    for part in range(2):
        peers[0][part].start()
        keep[part].start()
    shares[0].wait_recv()
    shares[4].start()
    peers[3][0].start()
    shares[3].wait_recv()
    shares[5].start()
    peers[1][1].start()
    shares[1].wait_recv()
    peers[3][1].start()
    shares[2].wait_recv()
    peers[1][0].start()
    shares[4].wait_recv()
    peers[2][0].start()
    shares[5].wait_recv()
    peers[2][1].start()
    for k in range(4):
        for part in range(2):
            peers[k][part].wait()
    for copy in core + hops + shares:
        copy.wait_send()
    for copy in keep:
        copy.wait()


def update(dense, table, accum):
    rows = dense.shape[0]
    ch = rows // 8
    hbm = pl.BlockSpec(memory_space=pl.ANY)
    dma = pltpu.SemaphoreType.DMA
    return pl.pallas_call(
        update_kernel,
        out_shape=jax.ShapeDtypeStruct((rows, 128), F32),
        in_specs=[hbm] * 3,
        out_specs=hbm,
        scratch_shapes=[
            pltpu.VMEM((4, ch, 128), F32),
            pltpu.VMEM((4, ch, 128), F32),
            pltpu.VMEM((6, ch // 2, 128), F32),
            pltpu.VMEM((ch, 128), F32),
            pltpu.VMEM((ch, 128), F32),
            pltpu.VMEM((ch, 128), F32),
            dma((8,)), dma((4,)), dma((4,)), dma((6,)), dma((6,)), dma((6,)), dma((6,)),
            dma((4, 2)), dma((4, 2)),
        ],
        compiler_params=pltpu.CompilerParams(
            vmem_limit_bytes=24 * MIB, collective_id=1, has_side_effects=True
        ),
        name="update",
    )(dense, table, accum)


def local(queries, positives, neg_ids, table, accum):
    ids, counts = dedup(neg_ids, table.shape[0])
    query_grad, received, arrived = exchange(ids, counts, queries, positives, table)
    dense = scatter(received, arrived, table.shape[0])
    return (update(dense, table, accum), query_grad)


def solution(mesh):
    return jax.shard_map(
        local,
        mesh=mesh,
        in_specs=(
            P(("dp", "own"), None),
            P(("dp", "own"), None),
            P(("dp", "own"), None),
            P("own", None),
            P("own", None),
        ),
        out_specs=(P("own", None), P(("dp", "own"), None)),
        check_vma=False,
    )
```

```python
import functools
import jax
import jax.numpy as jnp
from jax import lax
from jax.experimental import pallas as pl
from jax.experimental.pallas import tpu as pltpu
from jax.sharding import PartitionSpec as P

F32, BF16, I32 = jnp.float32, jnp.bfloat16, jnp.int32
LOG2E = 1.4426950408889634
MIB = 1024 * 1024
UPDATE_VMEM = 52
SCATTER_VMEM = 55


def split(x):
    hi = x.astype(BF16)
    return hi, (x - hi.astype(F32)).astype(BF16)


def dot(a, b):
    return lax.dot_general(a, b, (((1,), (0,)), ((), ())), preferred_element_type=F32)


def dot_t(a, b):
    return lax.dot_general(a, b, (((1,), (1,)), ((), ())), preferred_element_type=F32)


def dedup(rows_dev, ids_ref, out_ref, cnt_ref):
    owners, per = ids_ref.shape
    few = 256
    base = lax.broadcasted_iota(I32, (owners, per), 0) * rows_dev
    local = (ids_ref[...] - base).astype(F32)
    cols = jnp.transpose(jnp.concatenate([local, jnp.zeros((128 - owners, per), F32)], axis=0))
    lane = lax.broadcasted_iota(I32, (128, per), 1)
    sub = lax.broadcasted_iota(I32, (128, per), 0)
    firsts, counts = [], []
    for r in range(owners):
        row = local[r : r + 1, :]
        count = jnp.zeros((1, per), F32)
        before = jnp.zeros((1, per), F32)
        for b in range(per // 128):
            col = cols[b * 128 : (b + 1) * 128, r : r + 1]
            eq = jnp.where(col == row, 1.0, 0.0)
            count = count + jnp.sum(eq, axis=0, keepdims=True)
            before = before + jnp.sum(jnp.where(sub + b * 128 < lane, eq, 0.0), axis=0, keepdims=True)
        firsts.append(before < 0.5)
        counts.append(count)
    first = jnp.concatenate([jnp.where(f, 1.0, 0.0) for f in firsts], axis=0)
    count = jnp.concatenate(counts, axis=0)
    tri = jnp.where(
        lax.broadcasted_iota(I32, (per, per), 0) < lax.broadcasted_iota(I32, (per, per), 1), 1.0, 0.0
    ).astype(BF16)
    place = dot(first.astype(BF16), tri)
    place = jnp.where(first > 0.5, place, -1.0).astype(I32)
    li = local.astype(I32)
    ci = count.astype(I32)
    parts = [(li >> 7).astype(F32), (li & 127).astype(F32), (ci >> 4).astype(F32), (ci & 15).astype(F32)]
    slot = lax.broadcasted_iota(I32, (few, per), 0)
    for r in range(owners):
        hot = jnp.where(slot == place[r : r + 1, :], 1.0, 0.0).astype(BF16)
        vals = jnp.concatenate([p[r : r + 1, :] for p in parts] + [jnp.zeros((12, per), F32)], axis=0)
        got = dot_t(vals.astype(BF16), hot)
        ids = got[0:1, :] * 128.0 + got[1:2, :]
        cnt = got[2:3, :] * 16.0 + got[3:4, :]
        both = jnp.concatenate([ids[:, :128], ids[:, 128:], jnp.zeros((6, 128), F32)], axis=0)
        out_ref[r] = jnp.clip(both.astype(I32), 0, rows_dev - 1)
        cnt_ref[r] = jnp.broadcast_to(cnt, (8, few))


def scatter_kernel(ids_ref, grad_hbm, out_ref, grad_ref, sems):
    owners = grad_hbm.shape[0]

    def load(s):
        return pltpu.make_async_copy(grad_hbm.at[s], grad_ref.at[s], sems.at[s])

    def start(s, c):
        load(s).start()
        return c

    lax.fori_loop(0, owners, start, 0)
    out_ref[...] = jnp.zeros_like(out_ref)

    def half(s, h):
        for b in range(8):
            at = [pl.ds(ids_ref[s, h, b * 16 + i], 1) for i in range(16)]
            vals = [out_ref[at[i], :] + grad_ref[s, pl.ds(h * 128 + b * 16 + i, 1), :] for i in range(16)]
            for i in range(16):
                out_ref[at[i], :] = vals[i]

    def block(s, c):
        load(s).wait()
        lax.fori_loop(0, 2, lambda h, c: (half(s, h), c)[1], c)
        return c

    lax.fori_loop(0, owners, block, 0)


def scatter(ids, grads, rows_dev):
    return pl.pallas_call(
        scatter_kernel,
        out_shape=jax.ShapeDtypeStruct((rows_dev, 128), F32),
        in_specs=[pl.BlockSpec(memory_space=pltpu.SMEM), pl.BlockSpec(memory_space=pl.ANY)],
        out_specs=pl.BlockSpec(memory_space=pltpu.VMEM),
        scratch_shapes=[pltpu.VMEM(grads.shape, F32), pltpu.SemaphoreType.DMA((grads.shape[0],))],
        compiler_params=pltpu.CompilerParams(vmem_limit_bytes=SCATTER_VMEM * MIB),
        name="scatter",
    )(ids, grads)


def prepare(q_ref, p_ref, qtf, ptf, qt2, m, total, qacc):
    count = q_ref.shape[0]
    for t in range(count // 128):
        tile = pl.ds(t * 128, 128)
        qt = jnp.transpose(q_ref[tile, :])
        pt = jnp.transpose(p_ref[tile, :])
        qtf[:, tile] = qt
        ptf[:, tile] = pt
        hi, lo = split(qt * LOG2E)
        qt2[0:128, tile] = hi
        qt2[128:256, tile] = lo
        m[0:1, tile] = jnp.sum(qt * pt, axis=0, keepdims=True) * LOG2E
    total[...] = jnp.ones_like(total)
    qacc[...] = ptf[...]


def right_side(n):
    hi, lo = split(n)
    return jnp.concatenate([hi, hi], axis=1), jnp.concatenate([lo, lo], axis=1)


def left_side(n, w):
    nth, ntl = split(jnp.transpose(n) * w)
    wh, wl = split(w)
    sub = lax.broadcasted_iota(I32, (16, 256), 0)
    wrows = jnp.where(sub == 0, wh.astype(F32), jnp.where(sub == 1, wl.astype(F32), 0.0)).astype(BF16)
    return jnp.concatenate([nth, wrows, ntl], axis=0)


def score_tile(sides, tile, qt2, score, peak):
    right = qt2[:, tile]
    sc = dot(sides[0], right) + dot(sides[1], right)
    score[:, tile] = sc
    peak[0:1, tile] = jnp.max(sc, axis=0, keepdims=True)


def soft_tile(left, tile, s, score, peak, m, ms, total, qacc, eh, el):
    old = m[0:1, tile]
    new = jnp.maximum(old, peak[0:1, tile])
    alpha = jnp.exp2(old - new)
    m[0:1, tile] = new
    ms[s, 0:1, tile] = new
    h, l = split(jnp.exp2(score[:, tile] - new))
    eh[s, :, tile] = h
    el[s, :, tile] = l
    a1 = dot(left, h)
    a2 = dot(left[0:144], l)
    total[0:1, tile] = total[0:1, tile] * alpha + (a1[128:129] + a1[129:130]) + (a2[128:129] + a2[129:130])
    qacc[:, tile] = qacc[:, tile] * alpha + (a1[0:128] + (a1[144:272] + a2[0:128]))


def finish(qg_ref, ptf, m, total, qacc):
    count = qacc.shape[1]
    for t in range(count // 128):
        tile = pl.ds(t * 128, 128)
        g = qacc[:, tile] * (1.0 / total[0:1, tile]) - ptf[:, tile]
        qg_ref[tile, :] = jnp.transpose(g)


def phase_b(w, s, qtf, m, ms, total, eh, el):
    c = jnp.exp2(ms[s, 0:1, :] - m[0:1, :]) * (1.0 / total[0:1, :])
    qh, ql = split(qtf[...] * c)
    g1 = dot_t(eh[s], jnp.concatenate([qh, ql], axis=0))
    g2 = dot_t(el[s], qh)
    wc = jnp.transpose(jnp.broadcast_to(w, (128, 256)))
    return wc * (g1[:, 0:128] + (g1[:, 128:256] + g2))


def exchange_kernel(
    tq, raw_ref, q_hbm, p_hbm, table_hbm, accum_hbm,
    qg_ref, idr_ref, arrived_ref, tab_ref, acc_ref,
    ids_ref, cnt_ref, q_ref, p_ref, table_ref,
    qtf, ptf, qt2, m, ms, total, qacc, eh, el, score_a, score_b, peak_a, peak_b,
    idr, ids_smem, sent, rows, gsent, wslot,
    ids_s, ids_r, row_s, row_r, grad_s, grad_r, local_s,
):
    owners = raw_ref.shape[0]
    me = lax.axis_index("own")
    x, y = me // 4, me % 4

    def up(s):
        dx, dy = s % 4, (s + s // 4) % 4
        return ((x + dx) % 4) * 4 + (y + dy) % 4

    def down(s):
        dx, dy = s % 4, (s + s // 4) % 4
        return ((x + 4 - dx) % 4) * 4 + (y + 4 - dy) % 4

    def remote(src, dst, send, recv, device):
        return pltpu.make_async_remote_copy(
            src_ref=src, dst_ref=dst, send_sem=send, recv_sem=recv,
            device_id={"own": device}, device_id_type=pl.DeviceIdType.MESH,
        )

    def ids_copy(s):
        return remote(ids_ref.at[up(s)], idr.at[s], ids_s.at[s], ids_r.at[s], up(s))

    def row_copy(s):
        return remote(sent.at[s], rows.at[s], row_s.at[s], row_r.at[s], down(s))

    def grad_copy(s):
        return remote(gsent.at[s], arrived_ref.at[s], grad_s.at[s], grad_r.at[s], up(s))

    def each(first, body):
        def step(s, c):
            body(s)
            return c

        lax.fori_loop(first, owners, step, 0)

    load_q = pltpu.make_async_copy(q_hbm, q_ref, local_s.at[2])
    load_p = pltpu.make_async_copy(p_hbm, p_ref, local_s.at[3])
    load_table = pltpu.make_async_copy(table_hbm, table_ref, local_s.at[4])
    dp, ch = lax.axis_index("dp"), tab_ref.shape[0]
    share = pl.ds(pl.multiple_of((dp % 2 * 4 + dp // 2) * ch, ch), ch)
    keep_tab = pltpu.make_async_copy(table_hbm.at[share], tab_ref, local_s.at[5])
    keep_acc = pltpu.make_async_copy(accum_hbm.at[share], acc_ref, local_s.at[6])
    load_q.start()
    load_p.start()
    load_table.start()
    barrier = pltpu.get_barrier_semaphore()
    each(1, lambda s: pl.semaphore_signal(
        barrier, inc=1, device_id={"own": up(s)}, device_id_type=pl.DeviceIdType.MESH))
    dedup(table_ref.shape[0], raw_ref, ids_ref, cnt_ref)
    pl.semaphore_wait(barrier, owners - 1)
    each(1, lambda s: ids_copy(s).start())
    idr[0] = ids_ref[me]

    def counts(s):
        wslot[s] = cnt_ref[up(s)]

    each(0, counts)
    load_q.wait()
    load_p.wait()
    prepare(q_ref, p_ref, qtf, ptf, qt2, m, total, qacc)
    load_table.wait()
    each(1, lambda s: ids_copy(s).wait_recv())
    to_smem = pltpu.make_async_copy(idr, ids_smem, local_s.at[0])
    to_smem.start()
    idr_ref[...] = idr[...]
    to_smem.wait()

    def fetch(s, into):
        def half(h, c):
            for i in range(128):
                into[s, pl.ds(h * 128 + i, 1), :] = table_ref[pl.ds(ids_smem[s, h, i], 1), :]
            return c

        lax.fori_loop(0, 2, half, 0)

    def send_rows(s):
        fetch(s, sent)
        row_copy(s).start()

    each(1, send_rows)
    fetch(0, rows)
    keep_tab.start()
    keep_acc.start()
    sums = (m, ms, total, qacc, eh, el)
    tiles = [pl.ds(t * tq, tq) for t in range(q_ref.shape[0] // tq)]

    def both(s, score, peak, score_before, peak_before):
        row_copy(s).wait_recv()
        sides = right_side(rows[s])
        left = left_side(rows[s - 1], wslot[s - 1, 0:1, :])
        for tile in tiles:
            score_tile(sides, tile, qt2, score, peak)
            soft_tile(left, tile, s - 1, score_before, peak_before, *sums)

    own_sides = right_side(rows[0])
    for tile in tiles:
        score_tile(own_sides, tile, qt2, score_a, peak_a)

    def two(i, c):
        both(2 * i + 1, score_b, peak_b, score_a, peak_a)

        both(2 * i + 2, score_a, peak_a, score_b, peak_b)
        return c

    lax.fori_loop(0, owners // 2 - 1, two, 0)
    both(owners - 1, score_b, peak_b, score_a, peak_a)
    last = left_side(rows[owners - 1], wslot[owners - 1, 0:1, :])
    for tile in tiles:
        soft_tile(last, tile, owners - 1, score_b, peak_b, *sums)

    def gradients(i):
        s = (i + 1) % owners
        gsent[s] = phase_b(wslot[s, 0:1, :], s, qtf, m, ms, total, eh, el)

        @pl.when(s > 0)
        def _():
            grad_copy(s).start()

    each(0, gradients)
    own = pltpu.make_async_copy(gsent.at[0], arrived_ref.at[0], local_s.at[1])
    own.start()
    finish(qg_ref, ptf, m, total, qacc)
    each(1, lambda s: ids_copy(s).wait_send())
    each(1, lambda s: row_copy(s).wait_send())
    each(1, lambda s: grad_copy(s).wait())
    own.wait()
    keep_tab.wait()
    keep_acc.wait()


def exchange(ids, q, p, table, accum, tq=512):
    count, owners = q.shape[0], ids.shape[0]
    vm = pl.BlockSpec(memory_space=pltpu.VMEM)
    hbm = pl.BlockSpec(memory_space=pl.ANY)
    dma = pltpu.SemaphoreType.DMA((owners,))
    return pl.pallas_call(
        functools.partial(exchange_kernel, tq),
        out_shape=(
            jax.ShapeDtypeStruct((count, 128), F32),
            jax.ShapeDtypeStruct((owners, 8, 128), I32),
            jax.ShapeDtypeStruct((owners, 256, 128), F32),
            jax.ShapeDtypeStruct((table.shape[0] // 8, 128), F32),
            jax.ShapeDtypeStruct((table.shape[0] // 8, 128), F32),
        ),
        in_specs=[vm, hbm, hbm, hbm, hbm],
        out_specs=(vm, vm, hbm, hbm, hbm),
        scratch_shapes=[
            pltpu.VMEM((owners, 8, 128), I32),
            pltpu.VMEM((owners, 8, 256), F32),
            pltpu.VMEM((count, 128), F32),
            pltpu.VMEM((count, 128), F32),
            pltpu.VMEM(table.shape, F32),
            pltpu.VMEM((128, count), F32),
            pltpu.VMEM((128, count), F32),
            pltpu.VMEM((256, count), BF16),
            pltpu.VMEM((8, count), F32),
            pltpu.VMEM((owners, 8, count), F32),
            pltpu.VMEM((8, count), F32),
            pltpu.VMEM((128, count), F32),
            pltpu.VMEM((owners, 256, count), BF16),
            pltpu.VMEM((owners, 256, count), BF16),
            pltpu.VMEM((256, count), F32),
            pltpu.VMEM((256, count), F32),
            pltpu.VMEM((8, count), F32),
            pltpu.VMEM((8, count), F32),
            pltpu.VMEM((owners, 8, 128), I32),
            pltpu.SMEM((owners, 8, 128), I32),
            pltpu.VMEM((owners, 256, 128), F32),
            pltpu.VMEM((owners, 256, 128), F32),
            pltpu.VMEM((owners, 256, 128), F32),
            pltpu.VMEM((owners, 8, 256), F32),
        ]
        + [dma] * 6
        + [pltpu.SemaphoreType.DMA((7,))],
        compiler_params=pltpu.CompilerParams(
            vmem_limit_bytes=61 * MIB, collective_id=0, has_side_effects=True
        ),
        name="exchange",
    )(ids, q, p, table, accum)


def update_kernel(
    subs, d_ref, tab, acc, out_ref,
    mine, other, ring, fresh,
    load_s, core_s, core_r, ring_s, ring_r, all_s, all_r, peer_s, peer_r,
):
    rows = d_ref.shape[0]
    half, ch = rows // 2, rows // 8
    hf = ch // 2
    sz = hf // subs
    dp = lax.axis_index("dp")
    z, c = dp // 2, dp % 2
    peer = z * 2 + (1 - c)
    nxt = ((z + 1) % 4) * 2 + c
    prv = ((z + 3) % 4) * 2 + c

    def remote(src, dst, send, recv, device):
        return pltpu.make_async_remote_copy(
            src_ref=src, dst_ref=dst, send_sem=send, recv_sem=recv,
            device_id={"dp": device}, device_id_type=pl.DeviceIdType.MESH,
        )

    def at(k, core, part, j):
        first = core * half + ((z + k) % 4) * ch + part * hf + j * sz
        return pl.ds(pl.multiple_of(first, sz), sz)

    def rows_of(part, j):
        return pl.ds(part * hf + j * sz, sz)

    span = range(subs)
    pieces = [(2, 0), (2, 1), (1, 1), (3, 0), (1, 0), (3, 1), (0, 0), (0, 1)]
    order = [(k, part, j) for k, part in pieces for j in span]
    loads, core = {}, {}
    for n, (k, part, j) in enumerate(order):
        loads[k, part, j] = pltpu.make_async_copy(
            d_ref.at[at(k, c, part, j)], mine.at[k, rows_of(part, j)], load_s.at[n]
        )
        core[k, part, j] = remote(
            d_ref.at[at(k, 1 - c, part, j)], other.at[k, rows_of(part, j)], core_s.at[n], core_r.at[n], peer
        )
        loads[k, part, j].start()

    barrier = pltpu.get_barrier_semaphore()
    for device in (peer, nxt, prv):
        pl.semaphore_signal(barrier, inc=1, device_id={"dp": device}, device_id_type=pl.DeviceIdType.MESH)
    pl.semaphore_wait(barrier, 3)

    urgent = 2 * subs
    for piece in order[:urgent]:
        core[piece].start()

    def pair(k, part, j):
        loads[k, part, j].wait()
        core[k, part, j].wait_recv()
        r = rows_of(part, j)
        mine[k, r, :] = mine[k, r, :] + other[k, r, :]

    def hop(i, k, part, j, device):
        n = i * subs + j
        return remote(mine.at[k, rows_of(part, j)], ring.at[n], ring_s.at[n], ring_r.at[n], device)

    hops = [
        [hop(0, 2, 0, j, nxt) for j in span],
        [hop(1, 2, 1, j, prv) for j in span],
        [hop(2, 1, 1, j, nxt) for j in span],
        [hop(3, 3, 0, j, prv) for j in span],
        [hop(4, 1, 0, j, nxt) for j in span],
        [hop(5, 3, 1, j, prv) for j in span],
    ]
    for j in span:
        pair(2, 0, j)
        hops[0][j].start()
        pair(2, 1, j)
        hops[1][j].start()
    for piece in order[urgent:]:
        core[piece].start()
    for j in span:
        pair(1, 1, j)
        pair(3, 0, j)
    for j in span:
        hops[0][j].wait_send()
        hops[2][j].start()
        hops[1][j].wait_send()
        hops[3][j].start()
    for j in span:
        pair(1, 0, j)
        hops[0][j].wait_recv()
        r = rows_of(0, j)
        mine[1, r, :] = mine[1, r, :] + ring[j]
        hops[4][j].start()
        pair(3, 1, j)
        hops[1][j].wait_recv()
        r = rows_of(1, j)
        mine[3, r, :] = mine[3, r, :] + ring[subs + j]
        hops[5][j].start()
    for j in span:
        pair(0, 0, j)
        pair(0, 1, j)

    def adagrad(part, j, a, b):
        hops[a][j].wait_recv()
        hops[b][j].wait_recv()
        r = rows_of(part, j)
        grad = mine[0, r, :] + (ring[a * subs + j] + ring[b * subs + j])
        new_accum = acc[r, :] + grad * grad
        fresh[r, :] = tab[r, :] - 0.5 * grad / (jnp.sqrt(new_accum) + 1e-08)

    def own_part(i, part, j, device):
        n = i * subs + j
        return remote(fresh.at[rows_of(part, j)], out_ref.at[at(0, c, part, j)], all_s.at[n], all_r.at[n], device)

    def passed(i, k, part, j, device):
        n = i * subs + j
        r = at(k, c, part, j)
        return remote(out_ref.at[r], out_ref.at[r], all_s.at[n], all_r.at[n], device)

    def to_peer(k, part, j):
        n = (k * 2 + part) * subs + j
        r = at(k, c, part, j)
        src = fresh.at[rows_of(part, j)] if k == 0 else out_ref.at[r]
        return remote(src, out_ref.at[r], peer_s.at[n], peer_r.at[n], peer)

    shares = [
        [own_part(0, 0, j, nxt) for j in span],
        [own_part(1, 1, j, nxt) for j in span],
        [own_part(2, 0, j, prv) for j in span],
        [own_part(3, 1, j, prv) for j in span],
        [passed(4, 3, 0, j, nxt) for j in span],
        [passed(5, 1, 1, j, prv) for j in span],
    ]
    peers = [[[to_peer(k, part, j) for j in span] for part in range(2)] for k in range(4)]
    keep = []
    for j in span:
        adagrad(0, j, 3, 4)
        shares[0][j].start()
        adagrad(1, j, 2, 5)
        shares[3][j].start()
        shares[2][j].start()
        shares[1][j].start()
        for part in range(2):
            peers[0][part][j].start()
            keep.append(pltpu.make_async_copy(
                fresh.at[rows_of(part, j)], out_ref.at[at(0, c, part, j)], load_s.at[part * subs + j]))
            keep[-1].start()
    for j in span:
        shares[0][j].wait_recv()
        shares[4][j].start()
        peers[3][0][j].start()
        shares[3][j].wait_recv()
        shares[5][j].start()
        peers[1][1][j].start()
        shares[2][j].wait_recv()
        peers[1][0][j].start()
        shares[1][j].wait_recv()
        peers[3][1][j].start()
    for j in span:
        shares[4][j].wait_recv()
        peers[2][0][j].start()
        shares[5][j].wait_recv()
        peers[2][1][j].start()
    for copy in keep:
        copy.wait()
    for copies in hops[2:] + shares:
        for copy in copies:
            copy.wait_send()
    for k, part, j in order:
        core[k, part, j].wait_send()
        peers[k][part][j].wait()


def update(dense, tab, acc, subs=2):
    rows = dense.shape[0]
    ch = rows // 8
    hbm = pl.BlockSpec(memory_space=pl.ANY)
    vm = pl.BlockSpec(memory_space=pltpu.VMEM)
    dma = pltpu.SemaphoreType.DMA
    return pl.pallas_call(
        functools.partial(update_kernel, subs),
        out_shape=jax.ShapeDtypeStruct((rows, 128), F32),
        in_specs=[hbm, vm, vm],
        out_specs=hbm,
        scratch_shapes=[
            pltpu.VMEM((4, ch, 128), F32),
            pltpu.VMEM((4, ch, 128), F32),
            pltpu.VMEM((6 * subs, ch // 2 // subs, 128), F32),
            pltpu.VMEM((ch, 128), F32),
            dma((8 * subs,)),
            dma((8 * subs,)), dma((8 * subs,)),
            dma((6 * subs,)), dma((6 * subs,)),
            dma((6 * subs,)), dma((6 * subs,)),
            dma((8 * subs,)), dma((8 * subs,)),
        ],
        compiler_params=pltpu.CompilerParams(
            vmem_limit_bytes=UPDATE_VMEM * MIB, collective_id=1, has_side_effects=True
        ),
        name="update",
    )(dense, tab, acc)


def local(queries, positives, neg_ids, table, accum):
    query_grad, received, arrived, tab, acc = exchange(neg_ids, queries, positives, table, accum)
    dense = scatter(received, arrived, table.shape[0])
    return (update(dense, tab, acc), query_grad)


def solution(mesh):
    return jax.shard_map(
        local,
        mesh=mesh,
        in_specs=(
            P(("dp", "own"), None),
            P(("dp", "own"), None),
            P(("dp", "own"), None),
            P("own", None),
            P("own", None),
        ),
        out_specs=(P("own", None), P(("dp", "own"), None)),
        check_vma=False,
    )
```

```python
import functools
import jax
import jax.numpy as jnp
from jax import lax
from jax.experimental import pallas as pl
from jax.experimental.pallas import tpu as pltpu
from jax.sharding import PartitionSpec as P

F32, BF16, I32 = jnp.float32, jnp.bfloat16, jnp.int32
LOG2E = 1.4426950408889634
MIB = 1024 * 1024
UPDATE_VMEM = 48
SCATTER_VMEM = 55


def split(x):
    hi = x.astype(BF16)
    return hi, (x - hi.astype(F32)).astype(BF16)


def dot(a, b):
    return lax.dot_general(a, b, (((1,), (0,)), ((), ())), preferred_element_type=F32)


def dot_t(a, b):
    return lax.dot_general(a, b, (((1,), (1,)), ((), ())), preferred_element_type=F32)


def dedup(rows_dev, ids_ref, out_ref, cnt_ref):
    owners, per = ids_ref.shape
    few = 256
    base = lax.broadcasted_iota(I32, (owners, per), 0) * rows_dev
    local = (ids_ref[...] - base).astype(F32)
    cols = jnp.transpose(jnp.concatenate([local, jnp.zeros((128 - owners, per), F32)], axis=0))
    lane = lax.broadcasted_iota(I32, (128, per), 1)
    sub = lax.broadcasted_iota(I32, (128, per), 0)
    firsts, counts = [], []
    for r in range(owners):
        row = local[r : r + 1, :]
        count = jnp.zeros((1, per), F32)
        before = jnp.zeros((1, per), F32)
        for b in range(per // 128):
            col = cols[b * 128 : (b + 1) * 128, r : r + 1]
            eq = jnp.where(col == row, 1.0, 0.0)
            count = count + jnp.sum(eq, axis=0, keepdims=True)
            before = before + jnp.sum(jnp.where(sub + b * 128 < lane, eq, 0.0), axis=0, keepdims=True)
        firsts.append(before < 0.5)
        counts.append(count)
    first = jnp.concatenate([jnp.where(f, 1.0, 0.0) for f in firsts], axis=0)
    count = jnp.concatenate(counts, axis=0)
    tri = jnp.where(
        lax.broadcasted_iota(I32, (per, per), 0) < lax.broadcasted_iota(I32, (per, per), 1), 1.0, 0.0
    ).astype(BF16)
    place = dot(first.astype(BF16), tri)
    place = jnp.where(first > 0.5, place, -1.0).astype(I32)
    li = local.astype(I32)
    ci = count.astype(I32)
    parts = [(li >> 7).astype(F32), (li & 127).astype(F32), (ci >> 4).astype(F32), (ci & 15).astype(F32)]
    slot = lax.broadcasted_iota(I32, (few, per), 0)
    for r in range(owners):
        hot = jnp.where(slot == place[r : r + 1, :], 1.0, 0.0).astype(BF16)
        vals = jnp.concatenate([p[r : r + 1, :] for p in parts] + [jnp.zeros((12, per), F32)], axis=0)
        got = dot_t(vals.astype(BF16), hot)
        ids = got[0:1, :] * 128.0 + got[1:2, :]
        cnt = got[2:3, :] * 16.0 + got[3:4, :]
        both = jnp.concatenate([ids[:, :128], ids[:, 128:], jnp.zeros((6, 128), F32)], axis=0)
        out_ref[r] = jnp.clip(both.astype(I32), 0, rows_dev - 1)
        cnt_ref[r] = jnp.broadcast_to(cnt, (8, few))


def scatter_kernel(ids_ref, grad_hbm, out_ref, extra_ref, grad_ref, sems):
    owners = grad_hbm.shape[0]
    gap = owners // 2

    def load(s):
        return pltpu.make_async_copy(grad_hbm.at[s], grad_ref.at[s], sems.at[s])

    def start(s, c):
        load(s).start()
        load(s + gap).start()
        return c

    lax.fori_loop(0, gap, start, 0)
    out_ref[...] = jnp.zeros_like(out_ref)
    extra_ref[...] = jnp.zeros_like(extra_ref)

    def half(s, h):
        for b in range(8):
            at, vals = [], []
            for total, r in ((out_ref, s), (extra_ref, s + gap)):
                for i in range(16):
                    j = b * 16 + i
                    at.append(pl.ds(ids_ref[r, h, j], 1))
                    vals.append(total[at[-1], :] + grad_ref[r, pl.ds(h * 128 + j, 1), :])
            for i in range(16):
                out_ref[at[i], :] = vals[i]
                extra_ref[at[16 + i], :] = vals[16 + i]

    def block(s, c):
        load(s).wait()
        load(s + gap).wait()
        lax.fori_loop(0, 2, lambda h, c: (half(s, h), c)[1], c)
        return c

    lax.fori_loop(0, gap, block, 0)
    out_ref[...] = out_ref[...] + extra_ref[...]


def scatter(ids, grads, rows_dev):
    return pl.pallas_call(
        scatter_kernel,
        out_shape=jax.ShapeDtypeStruct((rows_dev, 128), F32),
        in_specs=[pl.BlockSpec(memory_space=pltpu.SMEM), pl.BlockSpec(memory_space=pl.ANY)],
        out_specs=pl.BlockSpec(memory_space=pltpu.VMEM),
        scratch_shapes=[
            pltpu.VMEM((rows_dev, 128), F32),
            pltpu.VMEM(grads.shape, F32),
            pltpu.SemaphoreType.DMA((grads.shape[0],)),
        ],
        compiler_params=pltpu.CompilerParams(vmem_limit_bytes=SCATTER_VMEM * MIB),
        name="scatter",
    )(ids, grads)


def prepare(q_ref, p_ref, qtf, ptf, qt2, m, total, qacc):
    count = q_ref.shape[0]
    for t in range(count // 128):
        tile = pl.ds(t * 128, 128)
        qt = jnp.transpose(q_ref[tile, :])
        pt = jnp.transpose(p_ref[tile, :])
        qtf[:, tile] = qt
        ptf[:, tile] = pt
        hi, lo = split(qt * LOG2E)
        qt2[0:128, tile] = hi
        qt2[128:256, tile] = lo
        m[0:1, tile] = jnp.sum(qt * pt, axis=0, keepdims=True) * LOG2E
    total[...] = jnp.ones_like(total)
    qacc[...] = ptf[...]


def right_side(n):
    hi, lo = split(n)
    return jnp.concatenate([hi, hi], axis=1), jnp.concatenate([lo, lo], axis=1)


def left_side(n, w):
    nth, ntl = split(jnp.transpose(n) * w)
    wh, wl = split(w)
    sub = lax.broadcasted_iota(I32, (16, 256), 0)
    wrows = jnp.where(sub == 0, wh.astype(F32), jnp.where(sub == 1, wl.astype(F32), 0.0)).astype(BF16)
    return jnp.concatenate([nth, wrows, ntl], axis=0)


def score_tile(sides, tile, qt2, score, peak):
    right = qt2[:, tile]
    sc = dot(sides[0], right) + dot(sides[1], right)
    score[:, tile] = sc
    peak[0:1, tile] = jnp.max(sc, axis=0, keepdims=True)


def soft_tile(left, tile, s, score, peak, m, ms, total, qacc, eh, el):
    old = m[0:1, tile]
    new = jnp.maximum(old, peak[0:1, tile])
    alpha = jnp.exp2(old - new)
    m[0:1, tile] = new
    ms[s, 0:1, tile] = new
    h, l = split(jnp.exp2(score[:, tile] - new))
    eh[s, :, tile] = h
    el[s, :, tile] = l
    a1 = dot(left, h)
    a2 = dot(left[0:144], l)
    total[0:1, tile] = total[0:1, tile] * alpha + (a1[128:129] + a1[129:130]) + (a2[128:129] + a2[129:130])
    qacc[:, tile] = qacc[:, tile] * alpha + (a1[0:128] + (a1[144:272] + a2[0:128]))


def finish(qg_ref, ptf, m, total, qacc):
    count = qacc.shape[1]
    for t in range(count // 128):
        tile = pl.ds(t * 128, 128)
        g = qacc[:, tile] * (1.0 / total[0:1, tile]) - ptf[:, tile]
        qg_ref[tile, :] = jnp.transpose(g)


def phase_b(w, s, qtf, m, ms, total, eh, el):
    c = jnp.exp2(ms[s, 0:1, :] - m[0:1, :]) * (1.0 / total[0:1, :])
    qh, ql = split(qtf[...] * c)
    g1 = dot_t(eh[s], jnp.concatenate([qh, ql], axis=0))
    g2 = dot_t(el[s], qh)
    wc = jnp.transpose(jnp.broadcast_to(w, (128, 256)))
    return wc * (g1[:, 0:128] + (g1[:, 128:256] + g2))


def exchange_kernel(
    tq, raw_ref, q_hbm, p_hbm, table_hbm, accum_hbm,
    qg_ref, idr_ref, arrived_ref, tab_ref, acc_ref,
    ids_ref, cnt_ref, q_ref, p_ref, table_ref,
    qtf, ptf, qt2, m, ms, total, qacc, eh, el, score_a, score_b, peak_a, peak_b,
    idr, ids_smem, sent, rows, gsent, wslot,
    ids_s, ids_r, row_s, row_r, grad_s, grad_r, local_s,
):
    owners = raw_ref.shape[0]
    me = lax.axis_index("own")
    x, y = me // 4, me % 4

    def up(s):
        dx, dy = s % 4, (s + s // 4) % 4
        return ((x + dx) % 4) * 4 + (y + dy) % 4

    def down(s):
        dx, dy = s % 4, (s + s // 4) % 4
        return ((x + 4 - dx) % 4) * 4 + (y + 4 - dy) % 4

    def remote(src, dst, send, recv, device):
        return pltpu.make_async_remote_copy(
            src_ref=src, dst_ref=dst, send_sem=send, recv_sem=recv,
            device_id={"own": device}, device_id_type=pl.DeviceIdType.MESH,
        )

    def ids_copy(s):
        return remote(ids_ref.at[up(s)], idr.at[s], ids_s.at[s], ids_r.at[s], up(s))

    def row_copy(s):
        return remote(sent.at[s], rows.at[s], row_s.at[s], row_r.at[s], down(s))

    def grad_copy(s):
        return remote(gsent.at[s], arrived_ref.at[s], grad_s.at[s], grad_r.at[s], up(s))

    def each(first, body):
        def step(s, c):
            body(s)
            return c

        lax.fori_loop(first, owners, step, 0)

    load_q = pltpu.make_async_copy(q_hbm, q_ref, local_s.at[2])
    load_p = pltpu.make_async_copy(p_hbm, p_ref, local_s.at[3])
    load_table = pltpu.make_async_copy(table_hbm, table_ref, local_s.at[4])
    dp, ch = lax.axis_index("dp"), tab_ref.shape[0]
    share = pl.ds(pl.multiple_of((dp % 2 * 4 + dp // 2) * ch, ch), ch)
    keep_tab = pltpu.make_async_copy(table_hbm.at[share], tab_ref, local_s.at[5])
    keep_acc = pltpu.make_async_copy(accum_hbm.at[share], acc_ref, local_s.at[6])
    load_q.start()
    load_p.start()
    load_table.start()
    barrier = pltpu.get_barrier_semaphore()
    each(1, lambda s: pl.semaphore_signal(
        barrier, inc=1, device_id={"own": up(s)}, device_id_type=pl.DeviceIdType.MESH))
    dedup(table_ref.shape[0], raw_ref, ids_ref, cnt_ref)
    pl.semaphore_wait(barrier, owners - 1)
    each(1, lambda s: ids_copy(s).start())
    idr[0] = ids_ref[me]

    def counts(s):
        wslot[s] = cnt_ref[up(s)]

    each(0, counts)
    load_q.wait()
    load_p.wait()
    prepare(q_ref, p_ref, qtf, ptf, qt2, m, total, qacc)
    load_table.wait()
    each(1, lambda s: ids_copy(s).wait_recv())
    to_smem = pltpu.make_async_copy(idr, ids_smem, local_s.at[0])
    to_smem.start()
    idr_ref[...] = idr[...]
    to_smem.wait()

    def fetch(s, into):
        def half(h, c):
            for b in range(128 // 32):
                got = [table_ref[pl.ds(ids_smem[s, h, b * 32 + i], 1), :] for i in range(32)]
                for i in range(32):
                    into[s, pl.ds(h * 128 + b * 32 + i, 1), :] = got[i]
            return c

        lax.fori_loop(0, 2, half, 0)

    def send_rows(s):
        fetch(s, sent)
        row_copy(s).start()

    each(1, send_rows)
    fetch(0, rows)
    keep_tab.start()
    keep_acc.start()
    sums = (m, ms, total, qacc, eh, el)
    tiles = [pl.ds(t * tq, tq) for t in range(q_ref.shape[0] // tq)]

    def both(s, score, peak, score_before, peak_before):
        row_copy(s).wait_recv()
        sides = right_side(rows[s])
        left = left_side(rows[s - 1], wslot[s - 1, 0:1, :])
        for tile in tiles:
            score_tile(sides, tile, qt2, score, peak)
            soft_tile(left, tile, s - 1, score_before, peak_before, *sums)

    own_sides = right_side(rows[0])
    for tile in tiles:
        score_tile(own_sides, tile, qt2, score_a, peak_a)

    def two(i, c):
        both(2 * i + 1, score_b, peak_b, score_a, peak_a)

        both(2 * i + 2, score_a, peak_a, score_b, peak_b)
        return c

    lax.fori_loop(0, owners // 2 - 1, two, 0)
    both(owners - 1, score_b, peak_b, score_a, peak_a)
    last = left_side(rows[owners - 1], wslot[owners - 1, 0:1, :])
    for tile in tiles:
        soft_tile(last, tile, owners - 1, score_b, peak_b, *sums)

    def gradients(i):
        s = (i + 1) % owners
        gsent[s] = phase_b(wslot[s, 0:1, :], s, qtf, m, ms, total, eh, el)

        @pl.when(s > 0)
        def _():
            grad_copy(s).start()

    each(0, gradients)
    own = pltpu.make_async_copy(gsent.at[0], arrived_ref.at[0], local_s.at[1])
    own.start()
    finish(qg_ref, ptf, m, total, qacc)
    each(1, lambda s: ids_copy(s).wait_send())
    each(1, lambda s: row_copy(s).wait_send())
    each(1, lambda s: grad_copy(s).wait())
    own.wait()
    keep_tab.wait()
    keep_acc.wait()


def exchange(ids, q, p, table, accum, tq=512):
    count, owners = q.shape[0], ids.shape[0]
    vm = pl.BlockSpec(memory_space=pltpu.VMEM)
    hbm = pl.BlockSpec(memory_space=pl.ANY)
    dma = pltpu.SemaphoreType.DMA((owners,))
    return pl.pallas_call(
        functools.partial(exchange_kernel, tq),
        out_shape=(
            jax.ShapeDtypeStruct((count, 128), F32),
            jax.ShapeDtypeStruct((owners, 8, 128), I32),
            jax.ShapeDtypeStruct((owners, 256, 128), F32),
            jax.ShapeDtypeStruct((table.shape[0] // 8, 128), F32),
            jax.ShapeDtypeStruct((table.shape[0] // 8, 128), F32),
        ),
        in_specs=[vm, hbm, hbm, hbm, hbm],
        out_specs=(vm, vm, hbm, vm, vm),
        scratch_shapes=[
            pltpu.VMEM((owners, 8, 128), I32),
            pltpu.VMEM((owners, 8, 256), F32),
            pltpu.VMEM((count, 128), F32),
            pltpu.VMEM((count, 128), F32),
            pltpu.VMEM(table.shape, F32),
            pltpu.VMEM((128, count), F32),
            pltpu.VMEM((128, count), F32),
            pltpu.VMEM((256, count), BF16),
            pltpu.VMEM((8, count), F32),
            pltpu.VMEM((owners, 8, count), F32),
            pltpu.VMEM((8, count), F32),
            pltpu.VMEM((128, count), F32),
            pltpu.VMEM((owners, 256, count), BF16),
            pltpu.VMEM((owners, 256, count), BF16),
            pltpu.VMEM((256, count), F32),
            pltpu.VMEM((256, count), F32),
            pltpu.VMEM((8, count), F32),
            pltpu.VMEM((8, count), F32),
            pltpu.VMEM((owners, 8, 128), I32),
            pltpu.SMEM((owners, 8, 128), I32),
            pltpu.VMEM((owners, 256, 128), F32),
            pltpu.VMEM((owners, 256, 128), F32),
            pltpu.VMEM((owners, 256, 128), F32),
            pltpu.VMEM((owners, 8, 256), F32),
        ]
        + [dma] * 6
        + [pltpu.SemaphoreType.DMA((7,))],
        compiler_params=pltpu.CompilerParams(
            vmem_limit_bytes=61 * MIB, collective_id=0, has_side_effects=True
        ),
        name="exchange",
    )(ids, q, p, table, accum)


def update_kernel(
    subs, d_ref, tab, acc, out_ref,
    mine, other, ring, fresh,
    load_s, core_s, core_r, ring_s, ring_r, all_s, all_r, peer_s, peer_r,
):
    rows = d_ref.shape[0]
    half, ch = rows // 2, rows // 8
    hf = ch // 2
    sz = hf // subs
    dp = lax.axis_index("dp")
    z, c = dp // 2, dp % 2
    peer = z * 2 + (1 - c)
    nxt = ((z + 1) % 4) * 2 + c
    prv = ((z + 3) % 4) * 2 + c

    def remote(src, dst, send, recv, device):
        return pltpu.make_async_remote_copy(
            src_ref=src, dst_ref=dst, send_sem=send, recv_sem=recv,
            device_id={"dp": device}, device_id_type=pl.DeviceIdType.MESH,
        )

    def at(k, core, part, j):
        first = core * half + ((z + k) % 4) * ch + part * hf + j * sz
        return pl.ds(pl.multiple_of(first, sz), sz)

    def rows_of(part, j):
        return pl.ds(part * hf + j * sz, sz)

    span = range(subs)
    pieces = [(2, 0), (2, 1), (1, 1), (3, 0), (1, 0), (3, 1), (0, 0), (0, 1)]
    order = [(k, part, j) for k, part in pieces for j in span]
    loads, core = {}, {}
    for n, (k, part, j) in enumerate(order):
        loads[k, part, j] = pltpu.make_async_copy(
            d_ref.at[at(k, c, part, j)], mine.at[k, rows_of(part, j)], load_s.at[n]
        )
        core[k, part, j] = remote(
            d_ref.at[at(k, 1 - c, part, j)], other.at[k, rows_of(part, j)], core_s.at[n], core_r.at[n], peer
        )
        loads[k, part, j].start()

    barrier = pltpu.get_barrier_semaphore()
    for device in (peer, nxt, prv):
        pl.semaphore_signal(barrier, inc=1, device_id={"dp": device}, device_id_type=pl.DeviceIdType.MESH)
    pl.semaphore_wait(barrier, 3)

    urgent = 2 * subs
    for piece in order[:urgent]:
        core[piece].start()

    def pair(k, part, j):
        loads[k, part, j].wait()
        core[k, part, j].wait_recv()
        r = rows_of(part, j)
        mine[k, r, :] = mine[k, r, :] + other[k, r, :]

    def hop(i, k, part, j, device):
        n = i * subs + j
        return remote(mine.at[k, rows_of(part, j)], ring.at[n], ring_s.at[n], ring_r.at[n], device)

    hops = [
        [hop(0, 2, 0, j, nxt) for j in span],
        [hop(1, 2, 1, j, prv) for j in span],
        [hop(2, 1, 1, j, nxt) for j in span],
        [hop(3, 3, 0, j, prv) for j in span],
        [hop(4, 1, 0, j, nxt) for j in span],
        [hop(5, 3, 1, j, prv) for j in span],
    ]
    for j in span:
        pair(2, 0, j)
        hops[0][j].start()
        pair(2, 1, j)
        hops[1][j].start()
    for piece in order[urgent:]:
        core[piece].start()
    for j in span:
        pair(1, 1, j)
        pair(3, 0, j)
    for j in span:
        hops[0][j].wait_send()
        hops[2][j].start()
        hops[1][j].wait_send()
        hops[3][j].start()
    for j in span:
        pair(1, 0, j)
        hops[0][j].wait_recv()
        r = rows_of(0, j)
        mine[1, r, :] = mine[1, r, :] + ring[j]
        hops[4][j].start()
        pair(3, 1, j)
        hops[1][j].wait_recv()
        r = rows_of(1, j)
        mine[3, r, :] = mine[3, r, :] + ring[subs + j]
        hops[5][j].start()
    for j in span:
        pair(0, 0, j)
        pair(0, 1, j)

    def adagrad(part, j, a, b):
        hops[a][j].wait_recv()
        hops[b][j].wait_recv()
        r = rows_of(part, j)
        grad = mine[0, r, :] + (ring[a * subs + j] + ring[b * subs + j])
        new_accum = acc[r, :] + grad * grad
        fresh[r, :] = tab[r, :] - 0.5 * grad / (jnp.sqrt(new_accum) + 1e-08)

    def own_part(i, part, j, device):
        n = i * subs + j
        return remote(fresh.at[rows_of(part, j)], out_ref.at[at(0, c, part, j)], all_s.at[n], all_r.at[n], device)

    def passed(i, k, part, j, device):
        n = i * subs + j
        r = at(k, c, part, j)
        return remote(out_ref.at[r], out_ref.at[r], all_s.at[n], all_r.at[n], device)

    def to_peer(k, part, j):
        n = (k * 2 + part) * subs + j
        r = at(k, c, part, j)
        src = fresh.at[rows_of(part, j)] if k == 0 else out_ref.at[r]
        return remote(src, out_ref.at[r], peer_s.at[n], peer_r.at[n], peer)

    shares = [
        [own_part(0, 0, j, nxt) for j in span],
        [own_part(1, 1, j, nxt) for j in span],
        [own_part(2, 0, j, prv) for j in span],
        [own_part(3, 1, j, prv) for j in span],
        [passed(4, 3, 0, j, nxt) for j in span],
        [passed(5, 1, 1, j, prv) for j in span],
    ]
    peers = [[[to_peer(k, part, j) for j in span] for part in range(2)] for k in range(4)]
    keep = []
    for j in span:
        adagrad(0, j, 3, 4)
        shares[0][j].start()
        adagrad(1, j, 2, 5)
        shares[3][j].start()
        shares[2][j].start()
        shares[1][j].start()
        for part in range(2):
            peers[0][part][j].start()
            keep.append(pltpu.make_async_copy(
                fresh.at[rows_of(part, j)], out_ref.at[at(0, c, part, j)], load_s.at[part * subs + j]))
            keep[-1].start()
    for j in span:
        shares[0][j].wait_recv()
        shares[4][j].start()
        peers[3][0][j].start()
        shares[3][j].wait_recv()
        shares[5][j].start()
        peers[1][1][j].start()
        shares[2][j].wait_recv()
        peers[1][0][j].start()
        shares[1][j].wait_recv()
        peers[3][1][j].start()
    for j in span:
        shares[4][j].wait_recv()
        peers[2][0][j].start()
        shares[5][j].wait_recv()
        peers[2][1][j].start()
    for copy in keep:
        copy.wait()
    for copies in hops[2:] + shares:
        for copy in copies:
            copy.wait_send()
    for k, part, j in order:
        core[k, part, j].wait_send()
        peers[k][part][j].wait()


def update(dense, tab, acc, subs=2):
    rows = dense.shape[0]
    ch = rows // 8
    hbm = pl.BlockSpec(memory_space=pl.ANY)
    vm = pl.BlockSpec(memory_space=pltpu.VMEM)
    dma = pltpu.SemaphoreType.DMA
    return pl.pallas_call(
        functools.partial(update_kernel, subs),
        out_shape=jax.ShapeDtypeStruct((rows, 128), F32),
        in_specs=[hbm, vm, vm],
        out_specs=hbm,
        scratch_shapes=[
            pltpu.VMEM((4, ch, 128), F32),
            pltpu.VMEM((4, ch, 128), F32),
            pltpu.VMEM((6 * subs, ch // 2 // subs, 128), F32),
            pltpu.VMEM((ch, 128), F32),
            dma((8 * subs,)),
            dma((8 * subs,)), dma((8 * subs,)),
            dma((6 * subs,)), dma((6 * subs,)),
            dma((6 * subs,)), dma((6 * subs,)),
            dma((8 * subs,)), dma((8 * subs,)),
        ],
        compiler_params=pltpu.CompilerParams(
            vmem_limit_bytes=UPDATE_VMEM * MIB, collective_id=1, has_side_effects=True
        ),
        name="update",
    )(dense, tab, acc)


def local(queries, positives, neg_ids, table, accum):
    query_grad, received, arrived, tab, acc = exchange(neg_ids, queries, positives, table, accum)
    dense = scatter(received, arrived, table.shape[0])
    return (update(dense, tab, acc), query_grad)


def solution(mesh):
    return jax.shard_map(
        local,
        mesh=mesh,
        in_specs=(
            P(("dp", "own"), None),
            P(("dp", "own"), None),
            P(("dp", "own"), None),
            P("own", None),
            P("own", None),
        ),
        out_specs=(P("own", None), P(("dp", "own"), None)),
        check_vma=False,
    )
```

```python
import functools
import jax
import jax.numpy as jnp
from jax import lax
from jax.experimental import pallas as pl
from jax.experimental.pallas import tpu as pltpu
from jax.sharding import PartitionSpec as P

F32, BF16, I32 = jnp.float32, jnp.bfloat16, jnp.int32
LOG2E = 1.4426950408889634
MIB = 1024 * 1024
UPDATE_VMEM = 48
SCATTER_VMEM = 55


def split(x):
    hi = x.astype(BF16)
    return hi, (x - hi.astype(F32)).astype(BF16)


def dot(a, b):
    return lax.dot_general(a, b, (((1,), (0,)), ((), ())), preferred_element_type=F32)


def dot_t(a, b):
    return lax.dot_general(a, b, (((1,), (1,)), ((), ())), preferred_element_type=F32)


def dedup(rows_dev, ids_ref, out_ref, cnt_ref):
    owners, per = ids_ref.shape
    few = 256
    base = lax.broadcasted_iota(I32, (owners, per), 0) * rows_dev
    local = (ids_ref[...] - base).astype(F32)
    cols = jnp.transpose(jnp.concatenate([local, jnp.zeros((128 - owners, per), F32)], axis=0))
    lane = lax.broadcasted_iota(I32, (128, per), 1)
    sub = lax.broadcasted_iota(I32, (128, per), 0)
    firsts, counts = [], []
    for r in range(owners):
        row = local[r : r + 1, :]
        count = jnp.zeros((1, per), F32)
        before = jnp.zeros((1, per), F32)
        for b in range(per // 128):
            col = cols[b * 128 : (b + 1) * 128, r : r + 1]
            eq = jnp.where(col == row, 1.0, 0.0)
            count = count + jnp.sum(eq, axis=0, keepdims=True)
            before = before + jnp.sum(jnp.where(sub + b * 128 < lane, eq, 0.0), axis=0, keepdims=True)
        firsts.append(before < 0.5)
        counts.append(count)
    first = jnp.concatenate([jnp.where(f, 1.0, 0.0) for f in firsts], axis=0)
    count = jnp.concatenate(counts, axis=0)
    tri = jnp.where(
        lax.broadcasted_iota(I32, (per, per), 0) < lax.broadcasted_iota(I32, (per, per), 1), 1.0, 0.0
    ).astype(BF16)
    place = dot(first.astype(BF16), tri)
    place = jnp.where(first > 0.5, place, -1.0).astype(I32)
    li = local.astype(I32)
    ci = count.astype(I32)
    parts = [(li >> 7).astype(F32), (li & 127).astype(F32), (ci >> 4).astype(F32), (ci & 15).astype(F32)]
    slot = lax.broadcasted_iota(I32, (few, per), 0)
    for r in range(owners):
        hot = jnp.where(slot == place[r : r + 1, :], 1.0, 0.0).astype(BF16)
        vals = jnp.concatenate([p[r : r + 1, :] for p in parts] + [jnp.zeros((12, per), F32)], axis=0)
        got = dot_t(vals.astype(BF16), hot)
        ids = got[0:1, :] * 128.0 + got[1:2, :]
        cnt = got[2:3, :] * 16.0 + got[3:4, :]
        both = jnp.concatenate([ids[:, :128], ids[:, 128:], jnp.zeros((6, 128), F32)], axis=0)
        out_ref[r] = jnp.clip(both.astype(I32), 0, rows_dev - 1)
        cnt_ref[r] = jnp.broadcast_to(cnt, (8, few))


def scatter_kernel(ids_ref, grad_hbm, out_ref, extra_ref, grad_ref, sems):
    owners = grad_hbm.shape[0]
    gap = owners // 2

    def load(s):
        return pltpu.make_async_copy(grad_hbm.at[s], grad_ref.at[s], sems.at[s])

    def start(s, c):
        load(s).start()
        load(s + gap).start()
        return c

    lax.fori_loop(0, gap, start, 0)
    out_ref[...] = jnp.zeros_like(out_ref)
    extra_ref[...] = jnp.zeros_like(extra_ref)

    def half(s, h):
        for b in range(8):
            at, vals = [], []
            for total, r in ((out_ref, s), (extra_ref, s + gap)):
                for i in range(16):
                    j = b * 16 + i
                    at.append(pl.ds(ids_ref[r, h, j], 1))
                    vals.append(total[at[-1], :] + grad_ref[r, pl.ds(h * 128 + j, 1), :])
            for i in range(16):
                out_ref[at[i], :] = vals[i]
                extra_ref[at[16 + i], :] = vals[16 + i]

    def block(s, c):
        load(s).wait()
        load(s + gap).wait()
        lax.fori_loop(0, 2, lambda h, c: (half(s, h), c)[1], c)
        return c

    lax.fori_loop(0, gap, block, 0)
    out_ref[...] = out_ref[...] + extra_ref[...]


def scatter(ids, grads, rows_dev):
    return pl.pallas_call(
        scatter_kernel,
        out_shape=jax.ShapeDtypeStruct((rows_dev, 128), F32),
        in_specs=[pl.BlockSpec(memory_space=pltpu.SMEM), pl.BlockSpec(memory_space=pl.ANY)],
        out_specs=pl.BlockSpec(memory_space=pltpu.VMEM),
        scratch_shapes=[
            pltpu.VMEM((rows_dev, 128), F32),
            pltpu.VMEM(grads.shape, F32),
            pltpu.SemaphoreType.DMA((grads.shape[0],)),
        ],
        compiler_params=pltpu.CompilerParams(vmem_limit_bytes=SCATTER_VMEM * MIB),
        name="scatter",
    )(ids, grads)


def prepare(q_ref, p_ref, qtf, ptf, qt2, m, total, qacc):
    count = q_ref.shape[0]
    for t in range(count // 128):
        tile = pl.ds(t * 128, 128)
        qt = jnp.transpose(q_ref[tile, :])
        pt = jnp.transpose(p_ref[tile, :])
        qtf[:, tile] = qt
        ptf[:, tile] = pt
        hi, lo = split(qt * LOG2E)
        qt2[0:128, tile] = hi
        qt2[128:256, tile] = lo
        m[0:1, tile] = jnp.sum(qt * pt, axis=0, keepdims=True) * LOG2E
    total[...] = jnp.ones_like(total)
    qacc[...] = ptf[...]


def right_side(n):
    hi, lo = split(n)
    return jnp.concatenate([hi, hi], axis=1), jnp.concatenate([lo, lo], axis=1)


def left_side(n, w):
    nth, ntl = split(jnp.transpose(n) * w)
    wh, wl = split(w)
    sub = lax.broadcasted_iota(I32, (16, 256), 0)
    wrows = jnp.where(sub == 0, wh.astype(F32), jnp.where(sub == 1, wl.astype(F32), 0.0)).astype(BF16)
    return jnp.concatenate([nth, wrows, ntl], axis=0)


def score_tile(sides, tile, qt2, score, peak):
    right = qt2[:, tile]
    sc = dot(sides[0], right) + dot(sides[1], right)
    score[:, tile] = sc
    peak[0:1, tile] = jnp.max(sc, axis=0, keepdims=True)


def soft_tile(left, tile, s, score, peak, m, ms, total, qacc, eh, el):
    old = m[0:1, tile]
    new = jnp.maximum(old, peak[0:1, tile])
    alpha = jnp.exp2(old - new)
    m[0:1, tile] = new
    ms[s, 0:1, tile] = new
    h, l = split(jnp.exp2(score[:, tile] - new))
    eh[s, :, tile] = h
    el[s, :, tile] = l
    a1 = dot(left, h)
    a2 = dot(left[0:144], l)
    total[0:1, tile] = total[0:1, tile] * alpha + (a1[128:129] + a1[129:130]) + (a2[128:129] + a2[129:130])
    qacc[:, tile] = qacc[:, tile] * alpha + (a1[0:128] + (a1[144:272] + a2[0:128]))


def finish(qg_ref, ptf, m, total, qacc):
    count = qacc.shape[1]
    for t in range(count // 128):
        tile = pl.ds(t * 128, 128)
        g = qacc[:, tile] * (1.0 / total[0:1, tile]) - ptf[:, tile]
        qg_ref[tile, :] = jnp.transpose(g)


def phase_b(w, s, qtf, m, ms, total, eh, el):
    c = jnp.exp2(ms[s, 0:1, :] - m[0:1, :]) * (1.0 / total[0:1, :])
    qh, ql = split(qtf[...] * c)
    g1 = dot_t(eh[s], jnp.concatenate([qh, ql], axis=0))
    g2 = dot_t(el[s], qh)
    wc = jnp.transpose(jnp.broadcast_to(w, (128, 256)))
    return wc * (g1[:, 0:128] + (g1[:, 128:256] + g2))


def exchange_kernel(
    tq, raw_ref, q_hbm, p_hbm, table_hbm, accum_hbm,
    qg_ref, idr_ref, arrived_ref, tab_ref, acc_ref,
    ids_ref, cnt_ref, q_ref, p_ref, table_ref,
    qtf, ptf, qt2, m, ms, total, qacc, eh, el, score_a, score_b, peak_a, peak_b,
    idr, ids_smem, sent, rows, gsent, wslot,
    ids_s, ids_r, row_s, row_r, grad_s, grad_r, local_s,
):
    owners = raw_ref.shape[0]
    me = lax.axis_index("own")
    x, y = me // 4, me % 4

    def up(s):
        t = 7 * s % owners
        dx, dy = t % 4, (t + t // 4) % 4
        return ((x + dx) % 4) * 4 + (y + dy) % 4

    def down(s):
        t = 7 * s % owners
        dx, dy = t % 4, (t + t // 4) % 4
        return ((x + 4 - dx) % 4) * 4 + (y + 4 - dy) % 4

    def remote(src, dst, send, recv, device):
        return pltpu.make_async_remote_copy(
            src_ref=src, dst_ref=dst, send_sem=send, recv_sem=recv,
            device_id={"own": device}, device_id_type=pl.DeviceIdType.MESH,
        )

    def ids_copy(s):
        return remote(ids_ref.at[up(s)], idr.at[s], ids_s.at[s], ids_r.at[s], up(s))

    def row_copy(s):
        return remote(sent.at[s], rows.at[s], row_s.at[s], row_r.at[s], down(s))

    def grad_copy(s):
        return remote(gsent.at[s], arrived_ref.at[s], grad_s.at[s], grad_r.at[s], up(s))

    def each(first, body):
        def step(s, c):
            body(s)
            return c

        lax.fori_loop(first, owners, step, 0)

    load_q = pltpu.make_async_copy(q_hbm, q_ref, local_s.at[2])
    load_p = pltpu.make_async_copy(p_hbm, p_ref, local_s.at[3])
    load_table = pltpu.make_async_copy(table_hbm, table_ref, local_s.at[4])
    dp, ch = lax.axis_index("dp"), tab_ref.shape[0]
    share = pl.ds(pl.multiple_of((dp % 2 * 4 + dp // 2) * ch, ch), ch)
    keep_tab = pltpu.make_async_copy(table_hbm.at[share], tab_ref, local_s.at[5])
    keep_acc = pltpu.make_async_copy(accum_hbm.at[share], acc_ref, local_s.at[6])
    load_q.start()
    load_p.start()
    load_table.start()
    barrier = pltpu.get_barrier_semaphore()
    each(1, lambda s: pl.semaphore_signal(
        barrier, inc=1, device_id={"own": up(s)}, device_id_type=pl.DeviceIdType.MESH))
    dedup(table_ref.shape[0], raw_ref, ids_ref, cnt_ref)
    pl.semaphore_wait(barrier, owners - 1)
    each(1, lambda s: ids_copy(s).start())
    idr[0] = ids_ref[me]

    def counts(s):
        wslot[s] = cnt_ref[up(s)]

    each(0, counts)
    load_q.wait()
    load_p.wait()
    prepare(q_ref, p_ref, qtf, ptf, qt2, m, total, qacc)
    load_table.wait()
    each(1, lambda s: ids_copy(s).wait_recv())
    to_smem = pltpu.make_async_copy(idr, ids_smem, local_s.at[0])
    to_smem.start()
    idr_ref[...] = idr[...]
    to_smem.wait()

    def fetch(s, into):
        def half(h, c):
            for b in range(128 // 32):
                got = [table_ref[pl.ds(ids_smem[s, h, b * 32 + i], 1), :] for i in range(32)]
                for i in range(32):
                    into[s, pl.ds(h * 128 + b * 32 + i, 1), :] = got[i]
            return c

        lax.fori_loop(0, 2, half, 0)

    def send_rows(s):
        fetch(s, sent)
        row_copy(s).start()

    each(1, send_rows)
    fetch(0, rows)
    keep_tab.start()
    keep_acc.start()
    sums = (m, ms, total, qacc, eh, el)
    tiles = [pl.ds(t * tq, tq) for t in range(q_ref.shape[0] // tq)]

    def both(s, score, peak, score_before, peak_before):
        row_copy(s).wait_recv()
        sides = right_side(rows[s])
        left = left_side(rows[s - 1], wslot[s - 1, 0:1, :])
        for tile in tiles:
            score_tile(sides, tile, qt2, score, peak)
            soft_tile(left, tile, s - 1, score_before, peak_before, *sums)

    own_sides = right_side(rows[0])
    for tile in tiles:
        score_tile(own_sides, tile, qt2, score_a, peak_a)

    def two(i, c):
        both(2 * i + 1, score_b, peak_b, score_a, peak_a)

        both(2 * i + 2, score_a, peak_a, score_b, peak_b)
        return c

    lax.fori_loop(0, owners // 2 - 1, two, 0)
    both(owners - 1, score_b, peak_b, score_a, peak_a)
    last = left_side(rows[owners - 1], wslot[owners - 1, 0:1, :])
    for tile in tiles:
        soft_tile(last, tile, owners - 1, score_b, peak_b, *sums)

    def gradients(i):
        s = (i + 1) % owners
        gsent[s] = phase_b(wslot[s, 0:1, :], s, qtf, m, ms, total, eh, el)

        @pl.when(s > 0)
        def _():
            grad_copy(s).start()

    each(0, gradients)
    own = pltpu.make_async_copy(gsent.at[0], arrived_ref.at[0], local_s.at[1])
    own.start()
    finish(qg_ref, ptf, m, total, qacc)
    each(1, lambda s: ids_copy(s).wait_send())
    each(1, lambda s: row_copy(s).wait_send())
    each(1, lambda s: grad_copy(s).wait())
    own.wait()
    keep_tab.wait()
    keep_acc.wait()


def exchange(ids, q, p, table, accum, tq=512):
    count, owners = q.shape[0], ids.shape[0]
    vm = pl.BlockSpec(memory_space=pltpu.VMEM)
    hbm = pl.BlockSpec(memory_space=pl.ANY)
    dma = pltpu.SemaphoreType.DMA((owners,))
    return pl.pallas_call(
        functools.partial(exchange_kernel, tq),
        out_shape=(
            jax.ShapeDtypeStruct((count, 128), F32),
            jax.ShapeDtypeStruct((owners, 8, 128), I32),
            jax.ShapeDtypeStruct((owners, 256, 128), F32),
            jax.ShapeDtypeStruct((table.shape[0] // 8, 128), F32),
            jax.ShapeDtypeStruct((table.shape[0] // 8, 128), F32),
        ),
        in_specs=[vm, hbm, hbm, hbm, hbm],
        out_specs=(vm, vm, hbm, vm, vm),
        scratch_shapes=[
            pltpu.VMEM((owners, 8, 128), I32),
            pltpu.VMEM((owners, 8, 256), F32),
            pltpu.VMEM((count, 128), F32),
            pltpu.VMEM((count, 128), F32),
            pltpu.VMEM(table.shape, F32),
            pltpu.VMEM((128, count), F32),
            pltpu.VMEM((128, count), F32),
            pltpu.VMEM((256, count), BF16),
            pltpu.VMEM((8, count), F32),
            pltpu.VMEM((owners, 8, count), F32),
            pltpu.VMEM((8, count), F32),
            pltpu.VMEM((128, count), F32),
            pltpu.VMEM((owners, 256, count), BF16),
            pltpu.VMEM((owners, 256, count), BF16),
            pltpu.VMEM((256, count), F32),
            pltpu.VMEM((256, count), F32),
            pltpu.VMEM((8, count), F32),
            pltpu.VMEM((8, count), F32),
            pltpu.VMEM((owners, 8, 128), I32),
            pltpu.SMEM((owners, 8, 128), I32),
            pltpu.VMEM((owners, 256, 128), F32),
            pltpu.VMEM((owners, 256, 128), F32),
            pltpu.VMEM((owners, 256, 128), F32),
            pltpu.VMEM((owners, 8, 256), F32),
        ]
        + [dma] * 6
        + [pltpu.SemaphoreType.DMA((7,))],
        compiler_params=pltpu.CompilerParams(
            vmem_limit_bytes=61 * MIB, collective_id=0, has_side_effects=True
        ),
        name="exchange",
    )(ids, q, p, table, accum)


def update_kernel(
    subs, d_ref, tab, acc, out_ref,
    mine, other, ring, fresh,
    load_s, core_s, core_r, ring_s, ring_r, all_s, all_r, peer_s, peer_r,
):
    rows = d_ref.shape[0]
    half, ch = rows // 2, rows // 8
    hf = ch // 2
    sz = hf // subs
    dp = lax.axis_index("dp")
    z, c = dp // 2, dp % 2
    peer = z * 2 + (1 - c)
    nxt = ((z + 1) % 4) * 2 + c
    prv = ((z + 3) % 4) * 2 + c

    def remote(src, dst, send, recv, device):
        return pltpu.make_async_remote_copy(
            src_ref=src, dst_ref=dst, send_sem=send, recv_sem=recv,
            device_id={"dp": device}, device_id_type=pl.DeviceIdType.MESH,
        )

    def at(k, core, part, j):
        first = core * half + ((z + k) % 4) * ch + part * hf + j * sz
        return pl.ds(pl.multiple_of(first, sz), sz)

    def rows_of(part, j):
        return pl.ds(part * hf + j * sz, sz)

    span = range(subs)
    pieces = [(2, 0), (2, 1), (1, 1), (3, 0), (1, 0), (3, 1), (0, 0), (0, 1)]
    order = [(k, part, j) for k, part in pieces for j in span]
    loads, core = {}, {}
    for n, (k, part, j) in enumerate(order):
        loads[k, part, j] = pltpu.make_async_copy(
            d_ref.at[at(k, c, part, j)], mine.at[k, rows_of(part, j)], load_s.at[n]
        )
        core[k, part, j] = remote(
            d_ref.at[at(k, 1 - c, part, j)], other.at[k, rows_of(part, j)], core_s.at[n], core_r.at[n], peer
        )
        loads[k, part, j].start()

    barrier = pltpu.get_barrier_semaphore()
    for device in (peer, nxt, prv):
        pl.semaphore_signal(barrier, inc=1, device_id={"dp": device}, device_id_type=pl.DeviceIdType.MESH)
    pl.semaphore_wait(barrier, 3)

    urgent = 2 * subs
    for piece in order[:urgent]:
        core[piece].start()

    def pair(k, part, j):
        loads[k, part, j].wait()
        core[k, part, j].wait_recv()
        r = rows_of(part, j)
        mine[k, r, :] = mine[k, r, :] + other[k, r, :]

    def hop(i, k, part, j, device):
        n = i * subs + j
        return remote(mine.at[k, rows_of(part, j)], ring.at[n], ring_s.at[n], ring_r.at[n], device)

    hops = [
        [hop(0, 2, 0, j, nxt) for j in span],
        [hop(1, 2, 1, j, prv) for j in span],
        [hop(2, 1, 1, j, nxt) for j in span],
        [hop(3, 3, 0, j, prv) for j in span],
        [hop(4, 1, 0, j, nxt) for j in span],
        [hop(5, 3, 1, j, prv) for j in span],
    ]
    for j in span:
        pair(2, 0, j)
        hops[0][j].start()
        pair(2, 1, j)
        hops[1][j].start()
    for piece in order[urgent:]:
        core[piece].start()
    for j in span:
        pair(1, 1, j)
        pair(3, 0, j)
    for j in span:
        hops[0][j].wait_send()
        hops[2][j].start()
        hops[1][j].wait_send()
        hops[3][j].start()
    for j in span:
        pair(1, 0, j)
        hops[0][j].wait_recv()
        r = rows_of(0, j)
        mine[1, r, :] = mine[1, r, :] + ring[j]
        hops[4][j].start()
        pair(3, 1, j)
        hops[1][j].wait_recv()
        r = rows_of(1, j)
        mine[3, r, :] = mine[3, r, :] + ring[subs + j]
        hops[5][j].start()
    for j in span:
        pair(0, 0, j)
        pair(0, 1, j)

    def adagrad(part, j, a, b):
        hops[a][j].wait_recv()
        hops[b][j].wait_recv()
        r = rows_of(part, j)
        grad = mine[0, r, :] + (ring[a * subs + j] + ring[b * subs + j])
        new_accum = acc[r, :] + grad * grad
        fresh[r, :] = tab[r, :] - 0.5 * grad / (jnp.sqrt(new_accum) + 1e-08)

    def own_part(i, part, j, device):
        n = i * subs + j
        return remote(fresh.at[rows_of(part, j)], out_ref.at[at(0, c, part, j)], all_s.at[n], all_r.at[n], device)

    def passed(i, k, part, j, device):
        n = i * subs + j
        r = at(k, c, part, j)
        return remote(out_ref.at[r], out_ref.at[r], all_s.at[n], all_r.at[n], device)

    def to_peer(k, part, j):
        n = (k * 2 + part) * subs + j
        r = at(k, c, part, j)
        src = fresh.at[rows_of(part, j)] if k == 0 else out_ref.at[r]
        return remote(src, out_ref.at[r], peer_s.at[n], peer_r.at[n], peer)

    shares = [
        [own_part(0, 0, j, nxt) for j in span],
        [own_part(1, 1, j, nxt) for j in span],
        [own_part(2, 0, j, prv) for j in span],
        [own_part(3, 1, j, prv) for j in span],
        [passed(4, 3, 0, j, nxt) for j in span],
        [passed(5, 1, 1, j, prv) for j in span],
    ]
    peers = [[[to_peer(k, part, j) for j in span] for part in range(2)] for k in range(4)]
    keep = []
    for j in span:
        adagrad(0, j, 3, 4)
        shares[0][j].start()
        adagrad(1, j, 2, 5)
        shares[3][j].start()
        shares[2][j].start()
        shares[1][j].start()
        for part in range(2):
            peers[0][part][j].start()
            keep.append(pltpu.make_async_copy(
                fresh.at[rows_of(part, j)], out_ref.at[at(0, c, part, j)], load_s.at[part * subs + j]))
            keep[-1].start()
    for j in span:
        shares[0][j].wait_recv()
        shares[4][j].start()
        peers[3][0][j].start()
        shares[3][j].wait_recv()
        shares[5][j].start()
        peers[1][1][j].start()
        shares[2][j].wait_recv()
        peers[1][0][j].start()
        shares[1][j].wait_recv()
        peers[3][1][j].start()
    for j in span:
        shares[4][j].wait_recv()
        peers[2][0][j].start()
        shares[5][j].wait_recv()
        peers[2][1][j].start()
    for copy in keep:
        copy.wait()
    for copies in hops[2:] + shares:
        for copy in copies:
            copy.wait_send()
    for k, part, j in order:
        core[k, part, j].wait_send()
        peers[k][part][j].wait()


def update(dense, tab, acc, subs=2):
    rows = dense.shape[0]
    ch = rows // 8
    hbm = pl.BlockSpec(memory_space=pl.ANY)
    vm = pl.BlockSpec(memory_space=pltpu.VMEM)
    dma = pltpu.SemaphoreType.DMA
    return pl.pallas_call(
        functools.partial(update_kernel, subs),
        out_shape=jax.ShapeDtypeStruct((rows, 128), F32),
        in_specs=[hbm, vm, vm],
        out_specs=hbm,
        scratch_shapes=[
            pltpu.VMEM((4, ch, 128), F32),
            pltpu.VMEM((4, ch, 128), F32),
            pltpu.VMEM((6 * subs, ch // 2 // subs, 128), F32),
            pltpu.VMEM((ch, 128), F32),
            dma((8 * subs,)),
            dma((8 * subs,)), dma((8 * subs,)),
            dma((6 * subs,)), dma((6 * subs,)),
            dma((6 * subs,)), dma((6 * subs,)),
            dma((8 * subs,)), dma((8 * subs,)),
        ],
        compiler_params=pltpu.CompilerParams(
            vmem_limit_bytes=UPDATE_VMEM * MIB, collective_id=1, has_side_effects=True
        ),
        name="update",
    )(dense, tab, acc)


def local(queries, positives, neg_ids, table, accum):
    query_grad, received, arrived, tab, acc = exchange(neg_ids, queries, positives, table, accum)
    dense = scatter(received, arrived, table.shape[0])
    return (update(dense, tab, acc), query_grad)


def solution(mesh):
    return jax.shard_map(
        local,
        mesh=mesh,
        in_specs=(
            P(("dp", "own"), None),
            P(("dp", "own"), None),
            P(("dp", "own"), None),
            P("own", None),
            P("own", None),
        ),
        out_specs=(P("own", None), P(("dp", "own"), None)),
        check_vma=False,
    )
```

```python
import functools
import jax
import jax.numpy as jnp
from jax import lax
from jax.experimental import pallas as pl
from jax.experimental.pallas import tpu as pltpu
from jax.sharding import PartitionSpec as P

F32, BF16, I32 = jnp.float32, jnp.bfloat16, jnp.int32
LOG2E = 1.4426950408889634
MIB = 1024 * 1024
UPDATE_VMEM = 48
SCATTER_VMEM = 55


def split(x):
    hi = x.astype(BF16)
    return hi, (x - hi.astype(F32)).astype(BF16)


def dot(a, b):
    return lax.dot_general(a, b, (((1,), (0,)), ((), ())), preferred_element_type=F32)


def dot_t(a, b):
    return lax.dot_general(a, b, (((1,), (1,)), ((), ())), preferred_element_type=F32)


def dedup(rows_dev, ids_ref, out_ref, cnt_ref):
    owners, per = ids_ref.shape
    few = 256
    base = lax.broadcasted_iota(I32, (owners, per), 0) * rows_dev
    local = (ids_ref[...] - base).astype(F32)
    cols = jnp.transpose(jnp.concatenate([local, jnp.zeros((128 - owners, per), F32)], axis=0))
    lane = lax.broadcasted_iota(I32, (128, per), 1)
    sub = lax.broadcasted_iota(I32, (128, per), 0)
    firsts, counts = [], []
    for r in range(owners):
        row = local[r : r + 1, :]
        count = jnp.zeros((1, per), F32)
        before = jnp.zeros((1, per), F32)
        for b in range(per // 128):
            col = cols[b * 128 : (b + 1) * 128, r : r + 1]
            eq = jnp.where(col == row, 1.0, 0.0)
            count = count + jnp.sum(eq, axis=0, keepdims=True)
            before = before + jnp.sum(jnp.where(sub + b * 128 < lane, eq, 0.0), axis=0, keepdims=True)
        firsts.append(before < 0.5)
        counts.append(count)
    first = jnp.concatenate([jnp.where(f, 1.0, 0.0) for f in firsts], axis=0)
    count = jnp.concatenate(counts, axis=0)
    tri = jnp.where(
        lax.broadcasted_iota(I32, (per, per), 0) < lax.broadcasted_iota(I32, (per, per), 1), 1.0, 0.0
    ).astype(BF16)
    place = dot(first.astype(BF16), tri)
    place = jnp.where(first > 0.5, place, -1.0).astype(I32)
    li = local.astype(I32)
    ci = count.astype(I32)
    parts = [(li >> 7).astype(F32), (li & 127).astype(F32), (ci >> 4).astype(F32), (ci & 15).astype(F32)]
    slot = lax.broadcasted_iota(I32, (few, per), 0)
    for r in range(owners):
        hot = jnp.where(slot == place[r : r + 1, :], 1.0, 0.0).astype(BF16)
        vals = jnp.concatenate([p[r : r + 1, :] for p in parts] + [jnp.zeros((12, per), F32)], axis=0)
        got = dot_t(vals.astype(BF16), hot)
        ids = got[0:1, :] * 128.0 + got[1:2, :]
        cnt = got[2:3, :] * 16.0 + got[3:4, :]
        both = jnp.concatenate([ids[:, :128], ids[:, 128:], jnp.zeros((6, 128), F32)], axis=0)
        out_ref[r] = jnp.clip(both.astype(I32), 0, rows_dev - 1)
        cnt_ref[r] = jnp.broadcast_to(cnt, (8, few))


def scatter_kernel(ids_ref, grad_hbm, qg_hbm, dense_hbm, qg_out, out_ref, extra_ref, grad_ref, qg_ref, sems, out_s, qg_s):
    owners = grad_hbm.shape[0]
    gap = owners // 2

    def load(s):
        return pltpu.make_async_copy(grad_hbm.at[s], grad_ref.at[s], sems.at[s])

    def start(s, c):
        load(s).start()
        load(s + gap).start()
        return c

    lax.fori_loop(0, gap, start, 0)
    qg_in = pltpu.make_async_copy(qg_hbm, qg_ref, qg_s.at[0])
    qg_in.start()
    out_ref[...] = jnp.zeros_like(out_ref)
    extra_ref[...] = jnp.zeros_like(extra_ref)
    qg_in.wait()
    qg_back = pltpu.make_async_copy(qg_ref, qg_out, qg_s.at[1])
    qg_back.start()

    def half(s, h):
        for b in range(8):
            at, vals = [], []
            for total, r in ((out_ref, s), (extra_ref, s + gap)):
                for i in range(16):
                    j = b * 16 + i
                    at.append(pl.ds(ids_ref[r, h, j], 1))
                    vals.append(total[at[-1], :] + grad_ref[r, pl.ds(h * 128 + j, 1), :])
            for i in range(16):
                out_ref[at[i], :] = vals[i]
                extra_ref[at[16 + i], :] = vals[16 + i]

    def block(s, c):
        load(s).wait()
        load(s + gap).wait()
        lax.fori_loop(0, 2, lambda h, c: (half(s, h), c)[1], c)
        return c

    lax.fori_loop(0, gap, block, 0)
    size = out_ref.shape[0] // 8
    parts = []
    for k in range(8):
        r = pl.ds(k * size, size)
        out_ref[r, :] = out_ref[r, :] + extra_ref[r, :]
        parts.append(pltpu.make_async_copy(out_ref.at[r], dense_hbm.at[r], out_s.at[k]))
        parts[k].start()
    for part in parts:
        part.wait()
    qg_back.wait()


def scatter(ids, grads, query_grad, rows_dev):
    hbm = pl.BlockSpec(memory_space=pl.ANY)
    return pl.pallas_call(
        scatter_kernel,
        out_shape=(
            jax.ShapeDtypeStruct((rows_dev, 128), F32),
            jax.ShapeDtypeStruct(query_grad.shape, F32),
        ),
        in_specs=[pl.BlockSpec(memory_space=pltpu.SMEM), hbm, hbm],
        out_specs=(hbm, hbm),
        scratch_shapes=[
            pltpu.VMEM((rows_dev, 128), F32),
            pltpu.VMEM((rows_dev, 128), F32),
            pltpu.VMEM(grads.shape, F32),
            pltpu.VMEM(query_grad.shape, F32),
            pltpu.SemaphoreType.DMA((grads.shape[0],)),
            pltpu.SemaphoreType.DMA((8,)),
            pltpu.SemaphoreType.DMA((2,)),
        ],
        compiler_params=pltpu.CompilerParams(vmem_limit_bytes=SCATTER_VMEM * MIB),
        name="scatter",
    )(ids, grads, query_grad)


def prepare(q_ref, p_ref, qtf, ptf, qt2, m, total, qacc):
    count = q_ref.shape[0]
    for t in range(count // 128):
        tile = pl.ds(t * 128, 128)
        qt = jnp.transpose(q_ref[tile, :])
        pt = jnp.transpose(p_ref[tile, :])
        qtf[:, tile] = qt
        ptf[:, tile] = pt
        hi, lo = split(qt * LOG2E)
        qt2[0:128, tile] = hi
        qt2[128:256, tile] = lo
        m[0:1, tile] = jnp.sum(qt * pt, axis=0, keepdims=True) * LOG2E
    total[...] = jnp.ones_like(total)
    qacc[...] = ptf[...]


def right_side(n):
    hi, lo = split(n)
    return jnp.concatenate([hi, hi], axis=1), jnp.concatenate([lo, lo], axis=1)


def left_side(n, w):
    nth, ntl = split(jnp.transpose(n) * w)
    wh, wl = split(w)
    sub = lax.broadcasted_iota(I32, (16, 256), 0)
    wrows = jnp.where(sub == 0, wh.astype(F32), jnp.where(sub == 1, wl.astype(F32), 0.0)).astype(BF16)
    return jnp.concatenate([nth, wrows, ntl], axis=0)


def score_tile(sides, tile, qt2, score, peak):
    right = qt2[:, tile]
    sc = dot(sides[0], right) + dot(sides[1], right)
    score[:, tile] = sc
    peak[0:1, tile] = jnp.max(sc, axis=0, keepdims=True)


def soft_tile(left, tile, s, score, peak, m, ms, total, qacc, eh, el):
    old = m[0:1, tile]
    new = jnp.maximum(old, peak[0:1, tile])
    alpha = jnp.exp2(old - new)
    m[0:1, tile] = new
    ms[s, 0:1, tile] = new
    h, l = split(jnp.exp2(score[:, tile] - new))
    eh[s, :, tile] = h
    el[s, :, tile] = l
    a1 = dot(left, h)
    a2 = dot(left[0:144], l)
    total[0:1, tile] = total[0:1, tile] * alpha + (a1[128:129] + a1[129:130]) + (a2[128:129] + a2[129:130])
    qacc[:, tile] = qacc[:, tile] * alpha + (a1[0:128] + (a1[144:272] + a2[0:128]))


def finish(qg_ref, ptf, m, total, qacc):
    count = qacc.shape[1]
    for t in range(count // 128):
        tile = pl.ds(t * 128, 128)
        g = qacc[:, tile] * (1.0 / total[0:1, tile]) - ptf[:, tile]
        qg_ref[tile, :] = jnp.transpose(g)


def phase_b(w, s, qtf, m, ms, total, eh, el):
    c = jnp.exp2(ms[s, 0:1, :] - m[0:1, :]) * (1.0 / total[0:1, :])
    qh, ql = split(qtf[...] * c)
    g1 = dot_t(eh[s], jnp.concatenate([qh, ql], axis=0))
    g2 = dot_t(el[s], qh)
    wc = jnp.transpose(jnp.broadcast_to(w, (128, 256)))
    return wc * (g1[:, 0:128] + (g1[:, 128:256] + g2))


def exchange_kernel(
    tq, raw_ref, q_hbm, p_hbm, table_hbm, accum_hbm,
    qg_ref, idr_ref, arrived_ref, tab_ref, acc_ref,
    ids_ref, cnt_ref, q_ref, p_ref, table_ref,
    qtf, ptf, qt2, m, ms, total, qacc, eh, el, score_a, score_b, peak_a, peak_b,
    idr, ids_smem, sent, rows, gsent, wslot,
    ids_s, ids_r, row_s, row_r, grad_s, grad_r, local_s,
):
    owners = raw_ref.shape[0]
    me = lax.axis_index("own")
    x, y = me // 4, me % 4

    def up(s):
        t = 7 * s % owners
        dx, dy = t % 4, (t + t // 4) % 4
        return ((x + dx) % 4) * 4 + (y + dy) % 4

    def down(s):
        t = 7 * s % owners
        dx, dy = t % 4, (t + t // 4) % 4
        return ((x + 4 - dx) % 4) * 4 + (y + 4 - dy) % 4

    def remote(src, dst, send, recv, device):
        return pltpu.make_async_remote_copy(
            src_ref=src, dst_ref=dst, send_sem=send, recv_sem=recv,
            device_id={"own": device}, device_id_type=pl.DeviceIdType.MESH,
        )

    def ids_copy(s):
        return remote(ids_ref.at[up(s)], idr.at[s], ids_s.at[s], ids_r.at[s], up(s))

    def row_copy(s):
        return remote(sent.at[s], rows.at[s], row_s.at[s], row_r.at[s], down(s))

    def grad_copy(s):
        return remote(gsent.at[s], arrived_ref.at[s], grad_s.at[s], grad_r.at[s], up(s))

    def each(first, body):
        def step(s, c):
            body(s)
            return c

        lax.fori_loop(first, owners, step, 0)

    load_q = pltpu.make_async_copy(q_hbm, q_ref, local_s.at[2])
    load_p = pltpu.make_async_copy(p_hbm, p_ref, local_s.at[3])
    load_table = pltpu.make_async_copy(table_hbm, table_ref, local_s.at[4])
    dp, ch = lax.axis_index("dp"), tab_ref.shape[0]
    share = pl.ds(pl.multiple_of((dp % 2 * 4 + dp // 2) * ch, ch), ch)
    keep_tab = pltpu.make_async_copy(table_hbm.at[share], tab_ref, local_s.at[5])
    keep_acc = pltpu.make_async_copy(accum_hbm.at[share], acc_ref, local_s.at[6])
    load_q.start()
    load_p.start()
    load_table.start()
    barrier = pltpu.get_barrier_semaphore()
    each(1, lambda s: pl.semaphore_signal(
        barrier, inc=1, device_id={"own": up(s)}, device_id_type=pl.DeviceIdType.MESH))
    dedup(table_ref.shape[0], raw_ref, ids_ref, cnt_ref)
    pl.semaphore_wait(barrier, owners - 1)
    each(1, lambda s: ids_copy(s).start())
    idr[0] = ids_ref[me]

    def counts(s):
        wslot[s] = cnt_ref[up(s)]

    each(0, counts)
    load_q.wait()
    load_p.wait()
    prepare(q_ref, p_ref, qtf, ptf, qt2, m, total, qacc)
    load_table.wait()
    each(1, lambda s: ids_copy(s).wait_recv())
    to_smem = pltpu.make_async_copy(idr, ids_smem, local_s.at[0])
    to_smem.start()
    idr_ref[...] = idr[...]
    to_smem.wait()

    def fetch(s, into):
        def half(h, c):
            for b in range(128 // 32):
                got = [table_ref[pl.ds(ids_smem[s, h, b * 32 + i], 1), :] for i in range(32)]
                for i in range(32):
                    into[s, pl.ds(h * 128 + b * 32 + i, 1), :] = got[i]
            return c

        lax.fori_loop(0, 2, half, 0)

    def send_rows(s):
        fetch(s, sent)
        row_copy(s).start()

    each(1, send_rows)
    fetch(0, rows)
    keep_tab.start()
    keep_acc.start()
    sums = (m, ms, total, qacc, eh, el)
    tiles = [pl.ds(t * tq, tq) for t in range(q_ref.shape[0] // tq)]

    def both(s, score, peak, score_before, peak_before):
        row_copy(s).wait_recv()
        sides = right_side(rows[s])
        left = left_side(rows[s - 1], wslot[s - 1, 0:1, :])
        for tile in tiles:
            score_tile(sides, tile, qt2, score, peak)
            soft_tile(left, tile, s - 1, score_before, peak_before, *sums)

    own_sides = right_side(rows[0])
    for tile in tiles:
        score_tile(own_sides, tile, qt2, score_a, peak_a)

    def two(i, c):
        both(2 * i + 1, score_b, peak_b, score_a, peak_a)

        both(2 * i + 2, score_a, peak_a, score_b, peak_b)
        return c

    lax.fori_loop(0, owners // 2 - 1, two, 0)
    both(owners - 1, score_b, peak_b, score_a, peak_a)
    last = left_side(rows[owners - 1], wslot[owners - 1, 0:1, :])
    for tile in tiles:
        soft_tile(last, tile, owners - 1, score_b, peak_b, *sums)

    def gradients(i):
        s = (i + 1) % owners
        gsent[s] = phase_b(wslot[s, 0:1, :], s, qtf, m, ms, total, eh, el)

        @pl.when(s > 0)
        def _():
            grad_copy(s).start()

    each(0, gradients)
    own = pltpu.make_async_copy(gsent.at[0], arrived_ref.at[0], local_s.at[1])
    own.start()
    finish(qg_ref, ptf, m, total, qacc)
    each(1, lambda s: ids_copy(s).wait_send())
    each(1, lambda s: row_copy(s).wait_send())
    each(1, lambda s: grad_copy(s).wait())
    own.wait()
    keep_tab.wait()
    keep_acc.wait()


def exchange(ids, q, p, table, accum, tq=512):
    count, owners = q.shape[0], ids.shape[0]
    vm = pl.BlockSpec(memory_space=pltpu.VMEM)
    hbm = pl.BlockSpec(memory_space=pl.ANY)
    dma = pltpu.SemaphoreType.DMA((owners,))
    return pl.pallas_call(
        functools.partial(exchange_kernel, tq),
        out_shape=(
            jax.ShapeDtypeStruct((count, 128), F32),
            jax.ShapeDtypeStruct((owners, 8, 128), I32),
            jax.ShapeDtypeStruct((owners, 256, 128), F32),
            jax.ShapeDtypeStruct((table.shape[0] // 8, 128), F32),
            jax.ShapeDtypeStruct((table.shape[0] // 8, 128), F32),
        ),
        in_specs=[vm, hbm, hbm, hbm, hbm],
        out_specs=(vm, vm, hbm, vm, vm),
        scratch_shapes=[
            pltpu.VMEM((owners, 8, 128), I32),
            pltpu.VMEM((owners, 8, 256), F32),
            pltpu.VMEM((count, 128), F32),
            pltpu.VMEM((count, 128), F32),
            pltpu.VMEM(table.shape, F32),
            pltpu.VMEM((128, count), F32),
            pltpu.VMEM((128, count), F32),
            pltpu.VMEM((256, count), BF16),
            pltpu.VMEM((8, count), F32),
            pltpu.VMEM((owners, 8, count), F32),
            pltpu.VMEM((8, count), F32),
            pltpu.VMEM((128, count), F32),
            pltpu.VMEM((owners, 256, count), BF16),
            pltpu.VMEM((owners, 256, count), BF16),
            pltpu.VMEM((256, count), F32),
            pltpu.VMEM((256, count), F32),
            pltpu.VMEM((8, count), F32),
            pltpu.VMEM((8, count), F32),
            pltpu.VMEM((owners, 8, 128), I32),
            pltpu.SMEM((owners, 8, 128), I32),
            pltpu.VMEM((owners, 256, 128), F32),
            pltpu.VMEM((owners, 256, 128), F32),
            pltpu.VMEM((owners, 256, 128), F32),
            pltpu.VMEM((owners, 8, 256), F32),
        ]
        + [dma] * 6
        + [pltpu.SemaphoreType.DMA((7,))],
        compiler_params=pltpu.CompilerParams(
            vmem_limit_bytes=61 * MIB, collective_id=0, has_side_effects=True
        ),
        name="exchange",
    )(ids, q, p, table, accum)


def update_kernel(
    subs, d_ref, tab, acc, out_ref,
    mine, other, ring, fresh,
    load_s, core_s, core_r, ring_s, ring_r, all_s, all_r, peer_s, peer_r,
):
    rows = d_ref.shape[0]
    half, ch = rows // 2, rows // 8
    hf = ch // 2
    sz = hf // subs
    dp = lax.axis_index("dp")
    z, c = dp // 2, dp % 2
    peer = z * 2 + (1 - c)
    nxt = ((z + 1) % 4) * 2 + c
    prv = ((z + 3) % 4) * 2 + c

    def remote(src, dst, send, recv, device):
        return pltpu.make_async_remote_copy(
            src_ref=src, dst_ref=dst, send_sem=send, recv_sem=recv,
            device_id={"dp": device}, device_id_type=pl.DeviceIdType.MESH,
        )

    def at(k, core, part, j):
        first = core * half + ((z + k) % 4) * ch + part * hf + j * sz
        return pl.ds(pl.multiple_of(first, sz), sz)

    def rows_of(part, j):
        return pl.ds(part * hf + j * sz, sz)

    span = range(subs)
    pieces = [(2, 0), (2, 1), (1, 1), (3, 0), (1, 0), (3, 1), (0, 0), (0, 1)]
    order = [(k, part, j) for k, part in pieces for j in span]
    loads, core = {}, {}
    for n, (k, part, j) in enumerate(order):
        loads[k, part, j] = pltpu.make_async_copy(
            d_ref.at[at(k, c, part, j)], mine.at[k, rows_of(part, j)], load_s.at[n]
        )
        core[k, part, j] = remote(
            d_ref.at[at(k, 1 - c, part, j)], other.at[k, rows_of(part, j)], core_s.at[n], core_r.at[n], peer
        )
        loads[k, part, j].start()

    barrier = pltpu.get_barrier_semaphore()
    for device in (peer, nxt, prv):
        pl.semaphore_signal(barrier, inc=1, device_id={"dp": device}, device_id_type=pl.DeviceIdType.MESH)
    pl.semaphore_wait(barrier, 3)

    urgent = 2 * subs
    for piece in order[:urgent]:
        core[piece].start()

    def pair(k, part, j):
        loads[k, part, j].wait()
        core[k, part, j].wait_recv()
        r = rows_of(part, j)
        mine[k, r, :] = mine[k, r, :] + other[k, r, :]

    def hop(i, k, part, j, device):
        n = i * subs + j
        return remote(mine.at[k, rows_of(part, j)], ring.at[n], ring_s.at[n], ring_r.at[n], device)

    hops = [
        [hop(0, 2, 0, j, nxt) for j in span],
        [hop(1, 2, 1, j, prv) for j in span],
        [hop(2, 1, 1, j, nxt) for j in span],
        [hop(3, 3, 0, j, prv) for j in span],
        [hop(4, 1, 0, j, nxt) for j in span],
        [hop(5, 3, 1, j, prv) for j in span],
    ]
    for j in span:
        pair(2, 0, j)
        hops[0][j].start()
        pair(2, 1, j)
        hops[1][j].start()
    for piece in order[urgent:]:
        core[piece].start()
    for j in span:
        pair(1, 1, j)
        pair(3, 0, j)
    for j in span:
        hops[0][j].wait_send()
        hops[2][j].start()
        hops[1][j].wait_send()
        hops[3][j].start()
    for j in span:
        pair(1, 0, j)
        hops[0][j].wait_recv()
        r = rows_of(0, j)
        mine[1, r, :] = mine[1, r, :] + ring[j]
        hops[4][j].start()
        pair(3, 1, j)
        hops[1][j].wait_recv()
        r = rows_of(1, j)
        mine[3, r, :] = mine[3, r, :] + ring[subs + j]
        hops[5][j].start()
    for j in span:
        pair(0, 0, j)
        pair(0, 1, j)

    def adagrad(part, j, a, b):
        hops[a][j].wait_recv()
        hops[b][j].wait_recv()
        r = rows_of(part, j)
        grad = mine[0, r, :] + (ring[a * subs + j] + ring[b * subs + j])
        new_accum = acc[r, :] + grad * grad
        fresh[r, :] = tab[r, :] - 0.5 * grad / (jnp.sqrt(new_accum) + 1e-08)

    def own_part(i, part, j, device):
        n = i * subs + j
        return remote(fresh.at[rows_of(part, j)], out_ref.at[at(0, c, part, j)], all_s.at[n], all_r.at[n], device)

    def passed(i, k, part, j, device):
        n = i * subs + j
        r = at(k, c, part, j)
        return remote(out_ref.at[r], out_ref.at[r], all_s.at[n], all_r.at[n], device)

    def to_peer(k, part, j):
        n = (k * 2 + part) * subs + j
        r = at(k, c, part, j)
        src = fresh.at[rows_of(part, j)] if k == 0 else out_ref.at[r]
        return remote(src, out_ref.at[r], peer_s.at[n], peer_r.at[n], peer)

    shares = [
        [own_part(0, 0, j, nxt) for j in span],
        [own_part(1, 1, j, nxt) for j in span],
        [own_part(2, 0, j, prv) for j in span],
        [own_part(3, 1, j, prv) for j in span],
        [passed(4, 3, 0, j, nxt) for j in span],
        [passed(5, 1, 1, j, prv) for j in span],
    ]
    peers = [[[to_peer(k, part, j) for j in span] for part in range(2)] for k in range(4)]
    keep = []
    for j in span:
        adagrad(0, j, 3, 4)
        shares[0][j].start()
        adagrad(1, j, 2, 5)
        shares[3][j].start()
        shares[2][j].start()
        shares[1][j].start()
        for part in range(2):
            peers[0][part][j].start()
            keep.append(pltpu.make_async_copy(
                fresh.at[rows_of(part, j)], out_ref.at[at(0, c, part, j)], load_s.at[part * subs + j]))
            keep[-1].start()
    for j in span:
        shares[0][j].wait_recv()
        shares[4][j].start()
        peers[3][0][j].start()
        shares[3][j].wait_recv()
        shares[5][j].start()
        peers[1][1][j].start()
        shares[2][j].wait_recv()
        peers[1][0][j].start()
        shares[1][j].wait_recv()
        peers[3][1][j].start()
    for j in span:
        shares[4][j].wait_recv()
        peers[2][0][j].start()
        shares[5][j].wait_recv()
        peers[2][1][j].start()
    for copy in keep:
        copy.wait()
    for copies in hops[2:] + shares:
        for copy in copies:
            copy.wait_send()
    for k, part, j in order:
        core[k, part, j].wait_send()
        peers[k][part][j].wait()


def update(dense, tab, acc, subs=2):
    rows = dense.shape[0]
    ch = rows // 8
    hbm = pl.BlockSpec(memory_space=pl.ANY)
    vm = pl.BlockSpec(memory_space=pltpu.VMEM)
    dma = pltpu.SemaphoreType.DMA
    return pl.pallas_call(
        functools.partial(update_kernel, subs),
        out_shape=jax.ShapeDtypeStruct((rows, 128), F32),
        in_specs=[hbm, vm, vm],
        out_specs=hbm,
        scratch_shapes=[
            pltpu.VMEM((4, ch, 128), F32),
            pltpu.VMEM((4, ch, 128), F32),
            pltpu.VMEM((6 * subs, ch // 2 // subs, 128), F32),
            pltpu.VMEM((ch, 128), F32),
            dma((8 * subs,)),
            dma((8 * subs,)), dma((8 * subs,)),
            dma((6 * subs,)), dma((6 * subs,)),
            dma((6 * subs,)), dma((6 * subs,)),
            dma((8 * subs,)), dma((8 * subs,)),
        ],
        compiler_params=pltpu.CompilerParams(
            vmem_limit_bytes=UPDATE_VMEM * MIB, collective_id=1, has_side_effects=True
        ),
        name="update",
    )(dense, tab, acc)


def local(queries, positives, neg_ids, table, accum):
    query_grad, received, arrived, tab, acc = exchange(neg_ids, queries, positives, table, accum)
    dense, query_grad = scatter(received, arrived, query_grad, table.shape[0])
    return (update(dense, tab, acc), query_grad)


def solution(mesh):
    return jax.shard_map(
        local,
        mesh=mesh,
        in_specs=(
            P(("dp", "own"), None),
            P(("dp", "own"), None),
            P(("dp", "own"), None),
            P("own", None),
            P("own", None),
        ),
        out_specs=(P("own", None), P(("dp", "own"), None)),
        check_vma=False,
    )
```
